256 devices in a mesh: store: 8 (over z_lo, core), prefill: 4 (over x), decode: 8 (over y, z_hi).
Axes of the slice: x: 4, y: 4, z: 8 (z_hi: 2, z_lo: 4; z = z_hi * 4 + z_lo), core: 2. Of those that a mesh axis runs over, the one named last changes fastest.
Arguments:
- prompt_q: bfloat16 [8, 512, 8192], P('decode', 'store', 'prefill'), may hold values from -180 to 180
- prompt_k: bfloat16 [8, 512, 1024], P('decode', 'store', 'prefill'), may hold values from -6 to 6
- prompt_v: bfloat16 [8, 512, 1024], P('decode', 'store', 'prefill'), may hold values from -6 to 6
- span_k: bfloat16 [128, 128, 1024], P(('store', 'decode'), None, 'prefill'), may hold values from -6 to 6
- span_v: bfloat16 [128, 128, 1024], P(('store', 'decode'), None, 'prefill'), may hold values from -6 to 6
- k_scale: bfloat16 [128, 8], P(('store', 'decode'), 'prefill'), may hold values from 0.25 to 2
- v_scale: bfloat16 [128, 8], P(('store', 'decode'), 'prefill'), may hold values from 0.25 to 2
- span_list: int32 [8, 28], replicated, may hold values from 0 to 127, all different within a row
- span_slot: int32 [128], replicated, may hold values from 0 to 127, each once
- span_count: int32 [8], replicated, may hold values from 1 to 28, as said below
- prompt_len: int32 [8], replicated, may hold values from 256 to 512, as said below
- decode_q: bfloat16 [8, 4, 8192], P(None, None, 'prefill'), may hold values from -180 to 180
- new_k: bfloat16 [8, 4, 1024], P(None, None, 'prefill'), may hold values from -6 to 6
- new_v: bfloat16 [8, 4, 1024], P(None, None, 'prefill'), may hold values from -6 to 6
- w_out: bfloat16 [8192, 8192], P('prefill', ('store', 'decode')), may hold values from -0.0625 to 0.0625
Outputs:
- prefill_out: float32 [8, 512, 8192], P('decode', 'store', 'prefill')
- decode_out: bfloat16 [32, 8192], P('prefill', ('store', 'decode'))
The draws below stay inside these ranges and needn't reach their ends.
Inputs may be any that keep to these rules, and one draw needn't show every extreme that they name: `span_list`: each row names distinct spans, and every span is named by some prompt. `span_slot`: each block holds exactly one span. `span_count`: some prompt uses all 28 slots. `prompt_len`: some prompt fills all 512 tokens.
All inputs are finite; a program needn't handle non-finite values.
Results may differ from the reference program's by a relative error of at most 0.015.
The reference program's roundings to bfloat16 on the way (of `decoded`) count: a program that leaves them out, or rounds other values in their place, can miss the bound.
Values may be sent and summed in bfloat16 or wider, within the bound.
No kernel may reach another device: no remote copies, remote signals or barrier semaphores. Data moves between devices by JAX's collectives and lax.ppermute only.
A program may use at most 128 MiB of HBM per device.

```python
import math
import jax
import jax.numpy as jnp
from jax import lax

D = 8192
H = 64
KVH = 8
HD = 128
GROUP = 8
BLOCK = 128
STEPS = 4
PLEN = 512
PROMPTS = 8
NBLK = 128
LIST = 28


def bounded_counts(key, size, low, high):
    values = jax.random.randint(key, (size,), low, high + 1)
    chosen = jax.random.randint(jax.random.fold_in(key, 7), (), 0, size)
    return jnp.where(jnp.arange(size) == chosen, high, values).astype(jnp.int32)


def draw_span_count(key, part):
    key = jax.random.fold_in(key, 11)
    return bounded_counts(key, PROMPTS, 1, LIST)


def draw_prompt_len(key, part):
    key = jax.random.fold_in(key, 12)
    return bounded_counts(key, PROMPTS, PLEN // 2, PLEN)


def draw_prompt_q(key, part):
    key = jax.random.fold_in(key, 13)
    base = jnp.clip(jax.random.normal(key, (PROMPTS, PLEN, H * HD), jnp.float32), -6.0, 6.0)
    return base.astype(jnp.bfloat16)


def draw_decode_q(key, part):
    key = jax.random.fold_in(key, 14)
    base = jnp.clip(jax.random.normal(key, (PROMPTS, STEPS, H * HD), jnp.float32), -6.0, 6.0)
    return base.astype(jnp.bfloat16)


def block_levels(own_key, extent, split, smallest, largest):
    level = 1.0
    for axis_at, parts in split:
        steps = jax.random.uniform(jax.random.fold_in(jax.random.fold_in(own_key, 6), axis_at), (parts,), jnp.float32, smallest / len(split), largest / len(split))
        level = level * jnp.repeat(jnp.exp(steps), extent[axis_at] // parts).reshape((-1,) + (1,) * (len(extent) - 1 - axis_at))
    return level


def choose_distinct(rng, rows, count, top, lift):
    order = jax.random.permutation(jax.random.fold_in(rng, 1), count)
    pull = order
    for power in range(3):
        pull = pull * pull // count
    pull = pull * lift // count
    chance = jax.random.randint(jax.random.fold_in(rng, 2), (rows, count), 0, 4096) + pull
    holders = jax.random.permutation(jax.random.fold_in(rng, 3), rows)[jnp.arange(count) % rows]
    chance = jnp.where(jnp.arange(rows)[:, None] == holders[None, :], 1 << 14, chance)
    merit = chance * count + jnp.arange(count)
    return lax.top_k(merit.astype(jnp.int32), top)[1].astype(jnp.int32)


def centred(key, extent, width, bound, pieces=(), kind=jnp.bfloat16):
    result = width * jax.random.normal(key, extent, jnp.float32)
    if pieces:
        result = result * block_levels(key, extent, pieces, -0.22, 0.18)
    return jnp.clip(result, -bound, bound).astype(kind)


def setup_inputs(seed: int = 0) -> dict:
    key_list = jax.random.split(jax.random.key(seed), 16)
    prompt_q = draw_prompt_q(jax.random.fold_in(key_list[15], 71), 0)
    prompt_k = centred(key_list[1], (PROMPTS, PLEN, KVH * HD), 1.0, 6.0, ((0, 8), (1, 8), (2, 4)))
    prompt_v = centred(key_list[2], (PROMPTS, PLEN, KVH * HD), 1.0, 6.0, ((0, 8), (1, 8), (2, 4)))
    span_k = centred(key_list[3], (NBLK, BLOCK, KVH * HD), 1.0, 6.0, ((0, 64), (2, 4)))
    span_v = centred(key_list[4], (NBLK, BLOCK, KVH * HD), 1.0, 6.0, ((0, 64), (2, 4)))
    k_scale = jnp.clip(jnp.exp(math.log(2.0) - 2.0794415 * jax.random.uniform(key_list[5], (NBLK, KVH), jnp.float32) ** block_levels(key_list[5], (NBLK, KVH), ((0, 64), (1, 4)), -0.2, 0.2)), 0.25, 2.0).astype(jnp.bfloat16)
    v_scale = jnp.clip(jnp.exp(math.log(2.0) - 2.0794415 * jax.random.uniform(key_list[6], (NBLK, KVH), jnp.float32) ** block_levels(key_list[6], (NBLK, KVH), ((0, 64), (1, 4)), -0.2, 0.2)), 0.25, 2.0).astype(jnp.bfloat16)
    span_list = choose_distinct(key_list[7], PROMPTS, NBLK, LIST, 3584)
    span_slot = jax.random.permutation(key_list[8], NBLK).astype(jnp.int32)
    span_count = draw_span_count(jax.random.fold_in(key_list[15], 71), 0)
    prompt_len = draw_prompt_len(jax.random.fold_in(key_list[15], 71), 0)
    decode_q = draw_decode_q(jax.random.fold_in(key_list[15], 71), 0)
    new_k = centred(key_list[12], (PROMPTS, STEPS, KVH * HD), 1.0, 6.0, ((2, 4),))
    new_v = centred(key_list[13], (PROMPTS, STEPS, KVH * HD), 1.0, 6.0, ((2, 4),))
    w_out = centred(key_list[14], (H * HD, D), (H * HD) ** -0.5, 0.0625, ((0, 4), (1, 64)))
    return {"prompt_q": prompt_q, "prompt_k": prompt_k, "prompt_v": prompt_v, "span_k": span_k, "span_v": span_v, "k_scale": k_scale, "v_scale": v_scale, "span_list": span_list, "span_slot": span_slot, "span_count": span_count, "prompt_len": prompt_len, "decode_q": decode_q, "new_k": new_k, "new_v": new_v, "w_out": w_out}


NEG = -1e+30

def dequant(codes, scales):
    count = codes.shape[0]
    wide = codes.reshape(count, codes.shape[1], KVH, HD).astype(jnp.float32) * scales.astype(jnp.float32)[:, None, :, None]
    return wide.astype(jnp.bfloat16).reshape(count * codes.shape[1], KVH, HD)

def attend(queries, keys, values, mask):
    scale = 1.0 / math.sqrt(HD)
    scores = jnp.einsum('rgd,kd->rgk', queries.astype(jnp.float32), keys.astype(jnp.float32)) * scale
    keep = mask[:, None, :]
    scores = jnp.where(keep, scores, NEG)
    peak = lax.optimization_barrier(jnp.max(scores, axis=2, keepdims=True))
    weights = jnp.where(keep, jnp.exp(scores - peak), 0.0)
    total = lax.optimization_barrier(jnp.sum(weights, axis=2))
    rounded = weights.astype(jnp.bfloat16)
    summed = jnp.einsum('rgk,kd->rgd', rounded.astype(jnp.float32), values.astype(jnp.float32))
    return summed / total[:, :, None]

def by_heads(queries, keys, values, mask):

    def one_head(head):
        return attend(queries[:, head], keys[:, head], values[:, head], mask)
    return lax.map(one_head, jnp.arange(KVH, dtype=jnp.int32))

def reference(prompt_q, prompt_k, prompt_v, span_k, span_v, k_scale, v_scale, span_list, span_slot, span_count, prompt_len, decode_q, new_k, new_v, w_out):

    def prompt_pass(index):
        slots = span_slot[span_list[index]].astype(jnp.int32)
        doc_keys = dequant(span_k[slots], k_scale[slots])
        doc_values = dequant(span_v[slots], v_scale[slots])
        doc_ok = jnp.repeat(jnp.arange(LIST, dtype=jnp.int32) < span_count[index], BLOCK)
        own_keys = prompt_k[index].reshape(PLEN, KVH, HD)
        own_values = prompt_v[index].reshape(PLEN, KVH, HD)
        position = jnp.arange(PLEN, dtype=jnp.int32)
        live = position < prompt_len[index]
        pre_mask = jnp.concatenate([jnp.broadcast_to(doc_ok[None, :], (PLEN, doc_ok.shape[0])), (position[None, :] <= position[:, None]) & live[None, :]], axis=1)
        keys = jnp.concatenate([doc_keys, own_keys], axis=0)
        values = jnp.concatenate([doc_values, own_values], axis=0)
        queries = prompt_q[index].reshape(PLEN, KVH, GROUP, HD)
        heads_out = by_heads(queries, keys, values, pre_mask)
        prefill_rows = jnp.transpose(heads_out, (1, 0, 2, 3)).reshape(PLEN, H * HD).astype(jnp.float32)
        step = jnp.arange(STEPS, dtype=jnp.int32)
        dec_mask = jnp.concatenate([jnp.broadcast_to(doc_ok[None, :], (STEPS, doc_ok.shape[0])), jnp.broadcast_to(live[None, :], (STEPS, PLEN)), step[None, :] <= step[:, None]], axis=1)
        dec_keys = jnp.concatenate([keys, new_k[index].reshape(STEPS, KVH, HD)], axis=0)
        dec_values = jnp.concatenate([values, new_v[index].reshape(STEPS, KVH, HD)], axis=0)
        dec_queries = decode_q[index].reshape(STEPS, KVH, GROUP, HD)
        dec_out = by_heads(dec_queries, dec_keys, dec_values, dec_mask)
        decoded = jnp.transpose(dec_out, (1, 0, 2, 3)).reshape(STEPS, H * HD).astype(jnp.bfloat16)
        return (prefill_rows, decoded)
    prefill_out, decoded = lax.map(prompt_pass, jnp.arange(PROMPTS, dtype=jnp.int32))
    decode_out = jnp.dot(decoded.reshape(PROMPTS * STEPS, H * HD), w_out, preferred_element_type=jnp.float32).astype(jnp.bfloat16)
    return (prefill_out, decode_out)
```

```python
import math

import jax
import jax.numpy as jnp
from jax import lax
from jax.experimental import pallas as pl
from jax.experimental.pallas import tpu as pltpu
from jax.sharding import Mesh, PartitionSpec as P

NEG = -1e30
HD = 128
UNIT = 16
VMEM = pl.BlockSpec(memory_space=pltpu.VMEM)
SMEM = pl.BlockSpec(memory_space=pltpu.SMEM)
LIMIT = 48 << 20
RANKS = ("hi", "lo", "y", "zh")
DECODE = ("y", "zh")
SWAP = [(0, 1), (1, 0)]


def params():
    return pltpu.CompilerParams(vmem_limit_bytes=LIMIT)


def spread_kernel(k_scale, v_scale, span_k, span_v, out):
    for kind, (codes, scale) in enumerate(((span_k, k_scale), (span_v, v_scale))):
        for block in range(codes.shape[0]):
            for head in range(2):
                part = codes[block, :, head * HD : (head + 1) * HD].astype(jnp.float32)
                part = (part * scale[block, head]).astype(jnp.bfloat16)
                out[head, kind, :, block] = part.reshape(-1, UNIT, HD)


def spread(span_k, span_v, k_scale, v_scale):
    blocks, rows, _ = span_k.shape
    return pl.pallas_call(
        spread_kernel,
        out_shape=jax.ShapeDtypeStruct((2, 2, rows // UNIT, blocks, UNIT, HD), jnp.bfloat16),
        in_specs=[SMEM, SMEM, VMEM, VMEM],
        out_specs=VMEM,
        compiler_params=params(),
    )(k_scale.astype(jnp.float32), v_scale.astype(jnp.float32), span_k, span_v)


def choose_kernel(core_ref, span_list, span_slot, mine, other, out):
    core = core_ref[0]
    for p in range(out.shape[0]):

        def one(t, carry):
            block = span_slot[span_list[p, 2 * t + core]]
            at = ((block >> 5) << 4) | (block & 15)
            here = ((block >> 4) & 1) == core

            @pl.when(here)
            def _():
                out[p, t] = mine[at]

            @pl.when(jnp.logical_not(here))
            def _():
                out[p, t] = other[at]

            return carry

        lax.fori_loop(0, out.shape[1], one, 0)


def choose(core, span_list, span_slot, mine, other):
    prompts, slots = span_list.shape
    return pl.pallas_call(
        choose_kernel,
        out_shape=jax.ShapeDtypeStruct((prompts, slots // 2, UNIT, HD), jnp.bfloat16),
        in_specs=[SMEM, SMEM, SMEM, VMEM, VMEM],
        out_specs=VMEM,
        compiler_params=params(),
    )(core, span_list, span_slot, mine, other)


COEF = math.log2(math.e) / math.sqrt(HD)


def scores_of(queries, keys):
    return lax.dot_general(
        queries, keys, (((1,), (1,)), ((), ())), preferred_element_type=jnp.float32
    )


def begin(scores, values):
    peak = jnp.max(scores, axis=1, keepdims=True)
    weights = jnp.exp2(scores * COEF - peak * COEF)
    total = jnp.sum(weights, axis=1, keepdims=True)
    accum = jnp.dot(weights.astype(jnp.bfloat16), values, preferred_element_type=jnp.float32)
    return peak, total, accum


def extend(state, scores, values):
    high, total, accum = state
    peak = jnp.maximum(high, jnp.max(scores, axis=1, keepdims=True))
    shrink = jnp.exp2((high - peak) * COEF)
    weights = jnp.exp2(scores * COEF - peak * COEF)
    total = total * shrink + jnp.sum(weights, axis=1, keepdims=True)
    accum = accum * shrink + jnp.dot(
        weights.astype(jnp.bfloat16), values, preferred_element_type=jnp.float32
    )
    return peak, total, accum


def doc_chunk(info, first, a, b, c, d):
    lo, core, count = info[1], info[2], info[3]
    width = 2 * (HD // UNIT) * UNIT

    def half(x):
        return x[:, pl.ds(first, 2)].reshape(width, HD)

    one = jnp.concatenate([half(a), half(b)], axis=0)
    two = jnp.concatenate([half(c), half(d)], axis=0)
    swap = jnp.full(one.shape, lo, jnp.int32) == 0
    keys = jnp.where(swap, one, two)
    values = jnp.where(swap, two, one)
    col = lax.broadcasted_iota(jnp.int32, (1, 2 * width), 1)
    owner = core ^ (col // width)
    slot = 2 * (first + ((col // UNIT) & 1)) + owner
    bias = jnp.where(slot < count, 0.0, NEG)
    return keys, values, bias


def prompt_positions(info):
    hi, lo, core = info[0], info[1], info[2]
    col = lax.broadcasted_iota(jnp.int32, (1, 512), 1)
    return (
        ((hi ^ ((col >> 6) & 1)) << 8)
        | ((lo ^ ((col >> 7) & 1)) << 7)
        | ((core ^ (col >> 8)) << 6)
        | (col & 63)
    )


def prefill_kernel(info, q, pkv, a, b, c, d, out, *, rows, far):
    hi, lo, core, count, length = info[0], info[1], info[2], info[3], info[4]
    tok = q.shape[0]
    group = q.shape[1] // HD
    step = rows // tok
    base = (((hi ^ far) << 2) | (lo << 1) | core) * tok
    kpos = prompt_positions(info)
    row = lax.broadcasted_iota(jnp.int32, (rows, 1), 0)
    qpos = base + (row & (tok - 1))
    keep = (kpos <= qpos) & (kpos < length)
    chunks = (count + 3) // 4
    pkeys = pkv[:, 0].reshape(512, HD)
    pvalues = pkv[:, 1].reshape(512, HD)
    for at in range(group // step):
        heads = [q[:, (at * step + g) * HD : (at * step + g + 1) * HD] for g in range(step)]
        queries = jnp.concatenate(heads, axis=0)
        state = begin(jnp.where(keep, scores_of(queries, pkeys), NEG), pvalues)

        def one(i, state):
            keys, values, bias = doc_chunk(info, 2 * i, a, b, c, d)
            return extend(state, scores_of(queries, keys) + bias, values)

        _, total, accum = lax.fori_loop(0, chunks, one, state)
        result = (accum / total).astype(out.dtype)
        for g in range(step):
            out[:, (at * step + g) * HD : (at * step + g + 1) * HD] = result[g * tok : (g + 1) * tok]


def decode_kernel(info, q, pkv, new_k, new_v, a, b, c, d, out, *, group):
    count, length = info[3], info[4]
    rows = q.shape[0]
    queries = q[...]
    kpos = prompt_positions(info)
    keep = jnp.broadcast_to(kpos < length, (rows, 512))
    scores = jnp.where(keep, scores_of(queries, pkv[:, 0].reshape(512, HD)), NEG)
    state = begin(scores, pkv[:, 1].reshape(512, HD))
    step = lax.broadcasted_iota(jnp.int32, (rows, HD), 0) // group
    col = lax.broadcasted_iota(jnp.int32, (rows, HD), 1)
    scores = jnp.where(col <= step, scores_of(queries, new_k[...]), NEG)
    state = extend(state, scores, new_v[...])

    def one(i, state):
        keys, values, bias = doc_chunk(info, 2 * i, a, b, c, d)
        return extend(state, scores_of(queries, keys) + bias, values)

    _, total, accum = lax.fori_loop(0, (count + 3) // 4, one, state)
    out[...] = (accum / total).astype(jnp.bfloat16)


def attend_cost(rows, keys):
    return pl.CostEstimate(
        flops=4 * rows * keys * HD, bytes_accessed=4 << 20, transcendentals=rows * keys
    )


def on_device(
    prompt_q,
    prompt_k,
    prompt_v,
    span_k,
    span_v,
    k_scale,
    v_scale,
    span_list,
    span_slot,
    span_count,
    prompt_len,
    decode_q,
    new_k,
    new_v,
    w_out,
):
    hi, lo, core = lax.axis_index("hi"), lax.axis_index("lo"), lax.axis_index("c")
    lane = lax.axis_index(DECODE)
    tok = prompt_q.shape[1]
    prompts, steps = decode_q.shape[:2]
    heads = prompt_q.shape[2] // HD // 2
    wide = heads * HD
    info = jnp.stack([hi, lo, core, span_count[lane], prompt_len[lane]]).astype(jnp.int32)

    def of_head(x, head, width):
        return lax.dynamic_slice_in_dim(x, head * width, width, x.ndim - 1)

    units = spread(span_k, span_v, k_scale, v_scale)
    units = units.reshape((-1,) + units.shape[3:])
    mine = lax.all_to_all(units, RANKS, 0, 0, tiled=True).reshape(-1, UNIT, HD)

    bundle = jnp.concatenate(
        [
            of_head(prompt_q[0], 1 - hi, wide),
            of_head(prompt_k[0], 1 - hi, HD),
            of_head(prompt_v[0], 1 - hi, HD),
        ],
        axis=1,
    )
    bundle = lax.ppermute(bundle, "hi", SWAP)
    far_q = bundle[:, :wide]
    near_q = of_head(prompt_q[0], hi, wide)
    near_k = of_head(prompt_k[0], hi, HD)
    near_v = of_head(prompt_v[0], hi, HD)
    pkv = jnp.stack([near_k, bundle[:, wide : wide + HD], near_v, bundle[:, wide + HD :]])
    pkv = pkv.reshape(1, 2, 2 * tok, HD)
    pkv = jnp.concatenate([pkv, lax.ppermute(pkv, "lo", SWAP)], axis=0)
    pkv = jnp.concatenate([pkv, lax.ppermute(pkv, "c", SWAP)], axis=0)

    other = lax.ppermute(mine, "c", SWAP)
    chosen = choose(core.reshape(1).astype(jnp.int32), span_list, span_slot, mine, other)
    a = lax.all_to_all(chosen, DECODE, 0, 0, tiled=True).reshape((prompts,) + chosen.shape[1:])
    c = lax.ppermute(a, "lo", SWAP)
    b = lax.ppermute(a, "c", SWAP)
    d = lax.ppermute(c, "c", SWAP)

    dq = of_head(lax.dynamic_index_in_dim(decode_q, lane, 0, keepdims=False), hi, wide)
    dq = dq.reshape(steps * heads, HD)

    def padded(x):
        x = of_head(lax.dynamic_index_in_dim(x, lane, 0, keepdims=False), hi, HD)
        return jnp.pad(x, ((0, HD - steps), (0, 0)))

    keys = a.shape[1] * 2 * HD + 8 * tok
    decoded = pl.pallas_call(
        lambda *refs: decode_kernel(*refs, group=heads),
        out_shape=jax.ShapeDtypeStruct((steps * heads, HD), jnp.bfloat16),
        in_specs=[SMEM] + [VMEM] * 8,
        out_specs=VMEM,
        compiler_params=params(),
        cost_estimate=attend_cost(steps * heads, keys),
    )(info, dq, pkv, padded(new_k), padded(new_v), a, b, c, d)
    decoded = decoded.reshape(1, steps, wide)
    both = jnp.concatenate([decoded, lax.ppermute(decoded, "hi", SWAP)], axis=2)
    attended = lax.all_to_all(
        jnp.broadcast_to(both, (prompts, steps, 2 * wide)), DECODE, 0, 0, tiled=True
    )
    attended = attended.reshape(prompts * steps, 2 * wide)

    def prefill(queries, far, dtype):
        return pl.pallas_call(
            lambda *refs: prefill_kernel(*refs, rows=256, far=far),
            out_shape=jax.ShapeDtypeStruct((tok, wide), dtype),
            in_specs=[SMEM] + [VMEM] * 6,
            out_specs=VMEM,
            compiler_params=params(),
            cost_estimate=attend_cost(tok * heads, keys),
        )(info, queries, pkv, a, b, c, d)

    far_out = lax.ppermute(prefill(far_q, 1, jnp.bfloat16), "hi", SWAP).astype(jnp.float32)
    near_out = prefill(near_q, 0, jnp.float32)
    first = hi == 0
    prefill_out = jnp.concatenate(
        [jnp.where(first, near_out, far_out), jnp.where(first, far_out, near_out)], axis=1
    )[None]

    w_near = lax.dynamic_slice_in_dim(w_out, hi * wide, wide, 0)
    w_far = lax.dynamic_slice_in_dim(w_out, (1 - hi) * wide, wide, 0)
    terms = jnp.dot(attended[:, :wide], w_near, preferred_element_type=jnp.float32) + jnp.dot(
        attended[:, wide:], w_far, preferred_element_type=jnp.float32
    )
    terms = lax.all_to_all(terms.reshape(4, -1, terms.shape[1]), "x", 0, 0, tiled=True)
    decode_out = jnp.sum(terms, axis=0).astype(jnp.bfloat16)
    return prefill_out, decode_out


def solution(mesh):
    fine = Mesh(mesh.devices.reshape(2, 2, 2, 4, 4, 2), ("hi", "lo", "c", "x", "y", "zh"))
    store = ("hi", "lo", "c")
    owners = store + DECODE
    placed = (
        P(DECODE, store, "x"),
        P(DECODE, store, "x"),
        P(DECODE, store, "x"),
        P(owners, None, "x"),
        P(owners, None, "x"),
        P(owners, "x"),
        P(owners, "x"),
        P(),
        P(),
        P(),
        P(),
        P(None, None, "x"),
        P(None, None, "x"),
        P(None, None, "x"),
        P("x", owners),
    )
    return jax.shard_map(
        on_device,
        mesh=fine,
        in_specs=placed,
        out_specs=(P(DECODE, store, "x"), P("x", owners)),
        check_vma=False,
    )
```

```python
import math

import jax
import jax.numpy as jnp
from jax import lax
from jax.experimental import pallas as pl
from jax.experimental.pallas import tpu as pltpu
from jax.sharding import Mesh, PartitionSpec as P

NEG = -1e30
HD = 128
GROUP = 8
UNIT = 16
VMEM = pl.BlockSpec(memory_space=pltpu.VMEM)
SMEM = pl.BlockSpec(memory_space=pltpu.SMEM)
RANKS = ("hi", "lo", "y", "zh")
DECODE = ("y", "zh")
SWAP = [(0, 1), (1, 0)]
COEF = math.log2(math.e) / math.sqrt(HD)
BF16 = jnp.bfloat16
F32 = jnp.float32


def params(limit=40):
    return pltpu.CompilerParams(vmem_limit_bytes=limit << 20)


def cost(us):
    return pl.CostEstimate(flops=int(us * 1.1e9), bytes_accessed=1 << 16, transcendentals=0)


def call(kernel, out_shape, in_specs, us, *args):
    return pl.pallas_call(
        kernel,
        out_shape=out_shape,
        in_specs=in_specs,
        out_specs=VMEM,
        compiler_params=params(),
        cost_estimate=cost(us),
    )(*args)


def whole(x):
    return pl.BlockSpec(x.shape, lambda i: (0,) * len(x.shape))


def single(kernel, out, scalars, us, args, scratch=(), limit=40):
    return pl.pallas_call(
        kernel,
        grid=(1,),
        out_shape=out,
        in_specs=[SMEM] * scalars + [whole(x) for x in args[scalars:]],
        out_specs=whole(out),
        scratch_shapes=list(scratch),
        compiler_params=params(limit),
        cost_estimate=cost(us),
    )(*args)


def lane_of_decode():
    return lax.axis_index("y") * 2 + lax.axis_index("zh")


def scores_of(queries, keys):
    return lax.dot_general(queries, keys, (((1,), (1,)), ((), ())), preferred_element_type=F32)


def iota(shape, dim):
    return lax.broadcasted_iota(jnp.int32, shape, dim)


def pack_kernel(q, k, v, out):
    other = 1 - lax.axis_index("hi")
    wide = GROUP * HD
    out[:, :wide] = q[0, :, pl.ds(pl.multiple_of(other * wide, wide), wide)]
    at = pl.ds(pl.multiple_of(other * HD, HD), HD)
    out[:, wide : wide + HD] = k[0, :, at]
    out[:, wide + HD :] = v[0, :, at]


def pair_kernel(k, v, bundle, out):
    at = pl.ds(pl.multiple_of(lax.axis_index("hi") * HD, HD), HD)
    wide = GROUP * HD
    out[0, 0] = k[0, :, at]
    out[1, 0] = v[0, :, at]
    out[0, 1] = bundle[:, wide : wide + HD]
    out[1, 1] = bundle[:, wide + HD :]


def spread_kernel(
    counts, lengths, k_scale, v_scale, span_k, span_v, prompt_k, prompt_v, span_list, span_slot, decode_q, new_k, new_v, out, fresh, dq
):
    tok = prompt_k.shape[1]
    prompts, steps = new_k.shape[:2]
    rows = prompts * steps
    lane = lane_of_decode()
    place = lax.axis_index("hi") * 4 + lax.axis_index("lo") * 2 + lax.axis_index("c")
    keys, values = [], []
    for kind, (codes, scale, full) in enumerate(((span_k, k_scale, keys), (span_v, v_scale, values))):
        factors = scale[...].astype(F32)
        for head in range(2):
            full.append([])
            for block in range(2):
                part = codes[block, :, head * HD : (head + 1) * HD].astype(F32)
                part = (part * factors[block : block + 1, head : head + 1]).astype(BF16)
                full[head].append(part)
                units = part.reshape(2, 4, UNIT, HD)
                for half in range(2):
                    for y in range(4):
                        out[head, half, 2 * y + kind, block] = units[half, y]
    for p in range(prompts):
        dq[p * steps : (p + 1) * steps] = decode_q[p].astype(F32)
    fresh[...] = jnp.zeros_like(fresh)
    fresh[0, 0:steps] = new_k[lane].astype(F32)
    fresh[1, 0:steps] = new_v[lane].astype(F32)
    width = 4 * HD
    row = iota((rows, 1), 0)
    prompt = row // steps
    step = row % steps
    listed = jnp.zeros((rows, span_list.shape[1]), jnp.int32)
    used = jnp.zeros((rows, 1), jnp.int32)
    for p in range(prompts):
        listed = jnp.where(prompt == p, span_list[p : p + 1, :], listed)
        used = jnp.where(prompt == p, counts[p], used)
    live = iota(listed.shape, 1) < used
    col = iota((rows, width), 1)
    slot = span_slot[...]
    first = (place * prompts + lane) * 2
    keep = jnp.zeros((rows, width), jnp.int32)
    for block in range(2):
        name = jnp.sum(jnp.where(slot == first + block, iota(slot.shape, 1), 0), axis=1, keepdims=True)
        has = jnp.max(jnp.where(live & (listed == name), 1, 0), axis=1, keepdims=True)
        keep = jnp.where((col >> 7) == block, has, keep)
    mine = jnp.where(prompt == lane, 1, 0)
    at = col - 2 * HD
    old = jnp.where((at >= 0) & (at < tok) & (place * tok + at < lengths[lane]), 1, 0)
    new = jnp.where((at >= HD) & (at - HD <= step) & (place == 0), 1, 0)
    keep = jnp.where(at >= 0, (old | new) * mine, keep)
    keep = (keep > 0)[None]
    for head in range(2):
        lanes = slice(head * HD, (head + 1) * HD)
        gap = jnp.zeros((HD - tok, HD), BF16)
        k_all = jnp.concatenate(keys[head] + [prompt_k[0, :, lanes], gap, fresh[0, :, lanes].astype(BF16)], axis=0)
        v_all = jnp.concatenate(values[head] + [prompt_v[0, :, lanes], gap, fresh[1, :, lanes].astype(BF16)], axis=0)
        base = head * GROUP
        queries = jnp.concatenate([dq[:, (base + g) * HD : (base + g + 1) * HD] for g in range(GROUP)], axis=0).astype(BF16)
        scores = scores_of(queries, k_all).reshape(GROUP, rows, width)
        scores = jnp.where(keep, scores, NEG) * COEF
        peak = jnp.max(scores, axis=2, keepdims=True)
        peak_hi = peak.astype(BF16).astype(F32)
        peak_lo = (peak - peak_hi).astype(BF16).astype(F32)
        weights = jnp.where(keep, jnp.exp2(scores - (peak_hi + peak_lo)), 0.0)
        total = jnp.sum(weights, axis=2, keepdims=True)
        total_hi = total.astype(BF16).astype(F32)
        total_lo = total - total_hi
        accum = jnp.dot(weights.reshape(GROUP * rows, width).astype(BF16), v_all, preferred_element_type=F32)
        accum = accum.astype(BF16).reshape(GROUP, 2, UNIT, HD)
        at = iota((GROUP, rows, HD), 2)
        stats = jnp.where(at == 0, peak_hi, jnp.where(at == 1, peak_lo, jnp.where(at == 2, total_hi, total_lo)))
        stats = jnp.where(at < 4, stats, 0.0).astype(BF16).reshape(GROUP, 2, UNIT, HD)
        for half in range(2):
            out[head, half, :, 2] = accum[:, half]
            out[head, half, :, 3] = stats[:, half]


def combine_kernel(mine, other, out):
    count = mine.shape[0]
    stats = jnp.concatenate([x[:, 3].reshape(count * UNIT, HD) for x in (mine, other)], axis=0)
    row, col = iota((HD, 2 * HD), 0), iota((HD, 2 * HD), 1)
    spread = jnp.where((row < 4) & ((row >> 1) == (col >> 7)), 1.0, 0.0).astype(BF16)
    stats = jnp.dot(stats, spread, preferred_element_type=F32)
    peaks = stats[:, :HD].reshape(2, count, UNIT, HD)
    totals = stats[:, HD:].reshape(2, count, UNIT, HD)
    share = jnp.exp2(peaks - jnp.max(peaks, axis=(0, 1), keepdims=True))
    total = jnp.sum(totals * share, axis=(0, 1))
    accum = jnp.sum(mine[:, 2].astype(F32) * share[0], axis=0) + jnp.sum(other[:, 2].astype(F32) * share[1], axis=0)
    out[...] = (accum / total).astype(BF16)


def choose_kernel(span_list, span_slot, mine, other, near, far, out, held):
    core, hi = lax.axis_index("c"), lax.axis_index("hi")
    slots = out.shape[1] - 2
    held[0] = mine[:, 0:2]
    held[1] = other[:, 0:2]
    for p in range(out.shape[0]):
        for t in range(slots):
            block = span_slot[span_list[p, 2 * t + core]]
            source = ((block >> 5) << 3) | ((block >> 1) & 7)
            out[p, t] = held[((block >> 4) & 1) ^ core, source, block & 1]
        out[p, slots + hi] = near[...]
        out[p, slots + 1 - hi] = far[...]


def begin(scores, values):
    peak = jnp.max(scores, axis=1, keepdims=True)
    weights = jnp.exp2(scores * COEF - peak * COEF)
    total = jnp.sum(weights, axis=1, keepdims=True)
    accum = jnp.dot(weights.astype(BF16), values, preferred_element_type=F32)
    return peak, total, accum


def extend(state, scores, values):
    high, total, accum = state
    peak = jnp.maximum(high, jnp.max(scores, axis=1, keepdims=True))
    shrink = jnp.exp2((high - peak) * COEF)
    weights = jnp.exp2(scores * COEF - peak * COEF)
    total = total * shrink + jnp.sum(weights, axis=1, keepdims=True)
    accum = accum * shrink + jnp.dot(weights.astype(BF16), values, preferred_element_type=F32)
    return peak, total, accum


PART = 4


def doc_rows(ref, kind, first):
    parts = [ref[2 * y + kind, pl.ds(first, PART)].reshape(PART * UNIT, HD) for y in range(4)]
    return jnp.concatenate(parts, axis=0)


def over_documents(queries, state, count, own, other):
    core = lax.axis_index("c")
    slots = own.shape[1] - 2
    col = iota((1, 8 * PART * UNIT), 1)
    parity = core ^ (col // (4 * PART * UNIT))
    turn = (col // UNIT) & (PART - 1)

    def one(i, state):
        first = jnp.minimum(PART * i, slots - PART)
        keys = jnp.concatenate([doc_rows(own, 0, first), doc_rows(other, 0, first)], axis=0)
        values = jnp.concatenate([doc_rows(own, 1, first), doc_rows(other, 1, first)], axis=0)
        at = first + turn
        bias = jnp.where((at >= PART * i) & (2 * at + parity < count), 0.0, NEG)
        return extend(state, scores_of(queries, keys) + bias, values)

    return lax.fori_loop(0, (count + 2 * PART - 1) // (2 * PART), one, state)


def queries_of(q, far):
    wide = GROUP * HD
    if far:
        heads = [q[:, g * HD : (g + 1) * HD] for g in range(GROUP)]
    else:
        base = lax.axis_index("hi") * wide
        heads = [q[0, :, pl.ds(pl.multiple_of(base + g * HD, HD), HD)] for g in range(GROUP)]
    return jnp.concatenate(heads, axis=0)


def first_kernel(counts, lengths, q, p0, p1, p2, p3, a, b, stats, sums, *, far):
    hi, lo, core = lax.axis_index("hi"), lax.axis_index("lo"), lax.axis_index("c")
    lane = lane_of_decode()
    count, length = counts[lane], lengths[lane]
    rows = sums.shape[0]
    tok = rows // GROUP
    col = iota((1, 8 * tok), 1)
    kpos = ((core ^ (col >> 8)) << 6) | ((lo ^ ((col >> 7) & 1)) << 7) | ((hi ^ ((col >> 6) & 1)) << 8) | (col & 63)
    row = iota((rows, 1), 0)
    pkeys = jnp.concatenate([x[0].reshape(2 * tok, HD) for x in (p0, p1, p2, p3)], axis=0)
    pvalues = jnp.concatenate([x[1].reshape(2 * tok, HD) for x in (p0, p1, p2, p3)], axis=0)
    queries = queries_of(q, far)
    qpos = (((hi ^ far) << 2) | (lo << 1) | core) * tok + (row & (tok - 1))
    keep = (kpos <= qpos) & (kpos < length)
    state = begin(jnp.where(keep, scores_of(queries, pkeys), NEG), pvalues)
    peak, total, accum = over_documents(queries, state, count, a, b)
    sums[...] = accum
    stats[0] = jnp.broadcast_to(peak, sums.shape)
    stats[1] = jnp.broadcast_to(total, sums.shape)


def last_kernel(counts, q, c, d, stats, sums, out, *, far):
    count = counts[lane_of_decode()]
    tok = out.shape[0]
    queries = queries_of(q, far)
    peak = jnp.max(stats[0], axis=1, keepdims=True)
    total = jnp.max(stats[1], axis=1, keepdims=True)
    state = (peak, total, sums[...])
    _, total, accum = over_documents(queries, state, count, c, d)
    result = (accum / total).astype(out.dtype)
    for g in range(GROUP):
        out[:, g * HD : (g + 1) * HD] = result[g * tok : (g + 1) * tok]


def project_kernel(own, swapped, w, out, held):
    lo, mine = lax.axis_index("lo"), lax.axis_index("x")

    def rows(x):
        return jnp.concatenate([x[g, head] for head in range(2) for g in range(GROUP)], axis=1)

    terms = jnp.dot(jnp.concatenate([rows(own), rows(swapped)], axis=0), w[...], preferred_element_type=F32)
    held[pl.ds(pl.multiple_of(lo * UNIT, UNIT), UNIT)] = terms[:UNIT]
    held[pl.ds(pl.multiple_of((1 - lo) * UNIT, UNIT), UNIT)] = terms[UNIT:]
    piece = out.shape[1]
    for k in range(4):
        out[k] = held[pl.ds(pl.multiple_of((mine ^ k) * piece, piece), piece)]


def on_device(
    prompt_q,
    prompt_k,
    prompt_v,
    span_k,
    span_v,
    k_scale,
    v_scale,
    span_list,
    span_slot,
    span_count,
    prompt_len,
    decode_q,
    new_k,
    new_v,
    w_out,
):
    hi = lax.axis_index("hi")
    tok = prompt_q.shape[1]
    prompts, steps = decode_q.shape[:2]
    slots = span_list.shape[1]
    wide = GROUP * HD
    shape = jax.ShapeDtypeStruct

    payload = single(
        spread_kernel,
        shape((2, 2, 8, 4, UNIT, HD), BF16),
        2,
        5,
        (
            span_count,
            prompt_len,
            k_scale,
            v_scale,
            span_k,
            span_v,
            prompt_k,
            prompt_v,
            span_list,
            span_slot.reshape(1, -1),
            decode_q,
            new_k,
            new_v,
        ),
        [pltpu.VMEM((2, HD, 2 * HD), F32), pltpu.VMEM((prompts * steps, decode_q.shape[2]), F32)],
        limit=60,
    )
    mine = lax.all_to_all(payload.reshape(32, 4, UNIT, HD), RANKS, 0, 0, tiled=True)
    bundle = single(pack_kernel, shape((tok, wide + 2 * HD), BF16), 0, 1.5, (prompt_q, prompt_k, prompt_v), limit=60)
    mine, bundle = lax.optimization_barrier((mine, bundle))
    bundle = lax.ppermute(bundle, "hi", SWAP)
    other = lax.ppermute(mine, "c", SWAP)

    done = call(combine_kernel, shape((UNIT, HD), BF16), [VMEM] * 2, 1, mine, other)
    chosen = pl.pallas_call(
        choose_kernel,
        out_shape=shape((prompts, slots // 2 + 2, UNIT, HD), BF16),
        in_specs=[SMEM] * 2 + [VMEM] * 4,
        out_specs=VMEM,
        scratch_shapes=[pltpu.VMEM((2, 32, 2, UNIT, HD), BF16)],
        compiler_params=params(),
        cost_estimate=cost(1),
    )(span_list, span_slot, mine, other, done, lax.ppermute(done, "hi", SWAP))
    chosen, bundle = lax.optimization_barrier((chosen, bundle))
    p0 = single(pair_kernel, shape((2, 2, tok, HD), BF16), 0, 1.5, (prompt_k, prompt_v, bundle))
    p1 = lax.ppermute(p0, "lo", SWAP)
    p2 = lax.ppermute(p0, "c", SWAP)
    p3 = lax.ppermute(p1, "c", SWAP)
    a = lax.all_to_all(chosen, DECODE, 0, 0, tiled=True)
    a, p1, p2, p3 = lax.optimization_barrier((a, p1, p2, p3))
    c = lax.ppermute(a, "lo", SWAP)
    b = lax.ppermute(a, "c", SWAP)

    def first(queries, is_far):
        return pl.pallas_call(
            lambda *refs: first_kernel(*refs, far=is_far),
            out_shape=(shape((2, GROUP * tok, HD), F32), shape((GROUP * tok, HD), F32)),
            in_specs=[SMEM] * 2 + [VMEM] * 7,
            out_specs=(VMEM, VMEM),
            compiler_params=params(),
            cost_estimate=cost(4),
        )(span_count, prompt_len, queries, p0, p1, p2, p3, a, b)

    def last(queries, is_far, dtype, state):
        return call(
            lambda *refs: last_kernel(*refs, far=is_far),
            shape((tok, wide), dtype),
            [SMEM] + [VMEM] * 5,
            4,
            span_count,
            queries,
            c,
            d,
            *state,
        )

    far_state, near_state = first(bundle, 1), first(prompt_q, 0)
    c, far_state, near_state = lax.optimization_barrier((c, far_state, near_state))
    d = lax.ppermute(c, "c", SWAP)

    lanes = a.shape[0]
    last_units = pl.BlockSpec((lanes, 2, UNIT, HD), lambda i: (0, slots // 4, 0, 0))
    terms = pl.pallas_call(
        project_kernel,
        out_shape=shape((4, prompts * steps // 4, w_out.shape[1]), F32),
        grid=(1,),
        in_specs=[last_units] * 2 + [whole(w_out)],
        out_specs=pl.BlockSpec((4, prompts * steps // 4, w_out.shape[1]), lambda i: (0, 0, 0)),
        scratch_shapes=[pltpu.VMEM((prompts * steps, w_out.shape[1]), F32)],
        compiler_params=params(),
        cost_estimate=cost(1),
    )(a, c, w_out)
    given = lax.ppermute(jnp.stack([terms[1], terms[3]]), "x", [(i, i ^ 1) for i in range(4)])
    far_out = last(bundle, 1, BF16, far_state)
    prompt_q, far_out, terms, given = lax.optimization_barrier((prompt_q, far_out, terms, given))
    far_out = lax.ppermute(far_out, "hi", SWAP)
    rest = lax.ppermute(terms[2] + given[1], "x", [(i, i ^ 2) for i in range(4)])
    near_out = last(prompt_q, 0, F32, near_state)
    decode_out = (terms[0] + given[0] + rest).astype(BF16)
    far_out = far_out.astype(F32)
    low = hi == 0
    prefill_out = jnp.concatenate(
        [jnp.where(low, near_out, far_out), jnp.where(low, far_out, near_out)], axis=1
    )[None]
    return prefill_out, decode_out


def solution(mesh):
    fine = Mesh(mesh.devices.reshape(2, 2, 2, 4, 4, 2), ("hi", "lo", "c", "x", "y", "zh"))
    store = ("hi", "lo", "c")
    owners = store + DECODE
    placed = (
        P(DECODE, store, "x"),
        P(DECODE, store, "x"),
        P(DECODE, store, "x"),
        P(owners, None, "x"),
        P(owners, None, "x"),
        P(owners, "x"),
        P(owners, "x"),
        P(),
        P(),
        P(),
        P(),
        P(None, None, "x"),
        P(None, None, "x"),
        P(None, None, "x"),
        P("x", owners),
    )
    return jax.shard_map(
        on_device,
        mesh=fine,
        in_specs=placed,
        out_specs=(P(DECODE, store, "x"), P("x", owners)),
        check_vma=False,
    )
```

```python
import math

import jax
import jax.numpy as jnp
from jax import lax
from jax.experimental import pallas as pl
from jax.experimental.pallas import tpu as pltpu
from jax.sharding import Mesh, PartitionSpec as P

NEG = -1e30
HD = 128
GROUP = 8
UNIT = 16
VMEM = pl.BlockSpec(memory_space=pltpu.VMEM)
SMEM = pl.BlockSpec(memory_space=pltpu.SMEM)
RANKS = ("hi", "lo", "y", "zh")
DECODE = ("y", "zh")
SWAP = [(0, 1), (1, 0)]
COEF = math.log2(math.e) / math.sqrt(HD)
BF16 = jnp.bfloat16
F32 = jnp.float32


def params(limit=40):
    return pltpu.CompilerParams(vmem_limit_bytes=limit << 20)


def cost(us):
    return pl.CostEstimate(flops=int(us * 1.1e9), bytes_accessed=1 << 16, transcendentals=0)


def call(kernel, out_shape, in_specs, us, *args):
    return pl.pallas_call(
        kernel,
        out_shape=out_shape,
        in_specs=in_specs,
        out_specs=VMEM,
        compiler_params=params(),
        cost_estimate=cost(us),
    )(*args)


def whole(x):
    return pl.BlockSpec(x.shape, lambda i: (0,) * len(x.shape))


def single(kernel, out, scalars, us, args, scratch=(), limit=40):
    return pl.pallas_call(
        kernel,
        grid=(1,),
        out_shape=out,
        in_specs=[SMEM] * scalars + [whole(x) for x in args[scalars:]],
        out_specs=whole(out),
        scratch_shapes=list(scratch),
        compiler_params=params(limit),
        cost_estimate=cost(us),
    )(*args)


def lane_of_decode():
    return lax.axis_index("y") * 2 + lax.axis_index("zh")


def scores_of(queries, keys):
    return lax.dot_general(queries, keys, (((1,), (1,)), ((), ())), preferred_element_type=F32)


def iota(shape, dim):
    return lax.broadcasted_iota(jnp.int32, shape, dim)


def pack_kernel(q, k, v, out):
    other = 1 - lax.axis_index("hi")
    wide = GROUP * HD
    out[:, :wide] = q[0, :, pl.ds(pl.multiple_of(other * wide, wide), wide)]
    at = pl.ds(pl.multiple_of(other * HD, HD), HD)
    out[:, wide : wide + HD] = k[0, :, at]
    out[:, wide + HD :] = v[0, :, at]


def pair_kernel(k, v, bundle, out):
    at = pl.ds(pl.multiple_of(lax.axis_index("hi") * HD, HD), HD)
    wide = GROUP * HD
    out[0, 0] = k[0, :, at]
    out[1, 0] = v[0, :, at]
    out[0, 1] = bundle[:, wide : wide + HD]
    out[1, 1] = bundle[:, wide + HD :]


def spread_kernel(
    counts, lengths, k_scale, v_scale, span_k, span_v, prompt_k, prompt_v, span_list, span_slot, decode_q, new_k, new_v, out, fresh, dq
):
    tok = prompt_k.shape[1]
    prompts, steps = new_k.shape[:2]
    rows = prompts * steps
    lane = lane_of_decode()
    place = lax.axis_index("hi") * 4 + lax.axis_index("lo") * 2 + lax.axis_index("c")
    keys, values = [], []
    for kind, (codes, scale, full) in enumerate(((span_k, k_scale, keys), (span_v, v_scale, values))):
        factors = scale[...].astype(F32)
        for head in range(2):
            full.append([])
            for block in range(2):
                part = codes[block, :, head * HD : (head + 1) * HD].astype(F32)
                part = (part * factors[block : block + 1, head : head + 1]).astype(BF16)
                full[head].append(part)
                units = part.reshape(2, 4, UNIT, HD)
                for half in range(2):
                    for y in range(4):
                        out[head, half, 2 * y + kind, block] = units[half, y]
    for p in range(prompts):
        dq[p * steps : (p + 1) * steps] = decode_q[p].astype(F32)
    fresh[...] = jnp.zeros_like(fresh)
    fresh[0, 0:steps] = new_k[lane].astype(F32)
    fresh[1, 0:steps] = new_v[lane].astype(F32)
    width = 4 * HD
    row = iota((rows, 1), 0)
    prompt = row // steps
    step = row % steps
    listed = jnp.zeros((rows, span_list.shape[1]), jnp.int32)
    used = jnp.zeros((rows, 1), jnp.int32)
    for p in range(prompts):
        listed = jnp.where(prompt == p, span_list[p : p + 1, :], listed)
        used = jnp.where(prompt == p, counts[p], used)
    live = iota(listed.shape, 1) < used
    col = iota((rows, width), 1)
    slot = span_slot[...]
    first = (place * prompts + lane) * 2
    keep = jnp.zeros((rows, width), jnp.int32)
    for block in range(2):
        name = jnp.sum(jnp.where(slot == first + block, iota(slot.shape, 1), 0), axis=1, keepdims=True)
        has = jnp.max(jnp.where(live & (listed == name), 1, 0), axis=1, keepdims=True)
        keep = jnp.where((col >> 7) == block, has, keep)
    mine = jnp.where(prompt == lane, 1, 0)
    at = col - 2 * HD
    old = jnp.where((at >= 0) & (at < tok) & (place * tok + at < lengths[lane]), 1, 0)
    new = jnp.where((at >= HD) & (at - HD <= step) & (place == 0), 1, 0)
    keep = jnp.where(at >= 0, (old | new) * mine, keep)
    keep = (keep > 0)[None]
    for head in range(2):
        lanes = slice(head * HD, (head + 1) * HD)
        gap = jnp.zeros((HD - tok, HD), BF16)
        k_all = jnp.concatenate(keys[head] + [prompt_k[0, :, lanes], gap, fresh[0, :, lanes].astype(BF16)], axis=0)
        v_all = jnp.concatenate(values[head] + [prompt_v[0, :, lanes], gap, fresh[1, :, lanes].astype(BF16)], axis=0)
        base = head * GROUP
        queries = jnp.concatenate([dq[:, (base + g) * HD : (base + g + 1) * HD] for g in range(GROUP)], axis=0).astype(BF16)
        scores = scores_of(queries, k_all).reshape(GROUP, rows, width)
        scores = jnp.where(keep, scores, NEG) * COEF
        peak = jnp.max(scores, axis=2, keepdims=True)
        peak_hi = peak.astype(BF16).astype(F32)
        peak_lo = (peak - peak_hi).astype(BF16).astype(F32)
        weights = jnp.where(keep, jnp.exp2(scores - (peak_hi + peak_lo)), 0.0)
        total = jnp.sum(weights, axis=2, keepdims=True)
        total_hi = total.astype(BF16).astype(F32)
        total_lo = total - total_hi
        accum = jnp.dot(weights.reshape(GROUP * rows, width).astype(BF16), v_all, preferred_element_type=F32)
        accum = accum.astype(BF16).reshape(GROUP, 2, UNIT, HD)
        at = iota((GROUP, rows, HD), 2)
        stats = jnp.where(at == 0, peak_hi, jnp.where(at == 1, peak_lo, jnp.where(at == 2, total_hi, total_lo)))
        stats = jnp.where(at < 4, stats, 0.0).astype(BF16).reshape(GROUP, 2, UNIT, HD)
        for half in range(2):
            out[head, half, :, 2] = accum[:, half]
            out[head, half, :, 3] = stats[:, half]


def combine_kernel(mine, other, out):
    count = mine.shape[0]
    stats = jnp.concatenate([x[:, 3].reshape(count * UNIT, HD) for x in (mine, other)], axis=0)
    row, col = iota((HD, 2 * HD), 0), iota((HD, 2 * HD), 1)
    spread = jnp.where((row < 4) & ((row >> 1) == (col >> 7)), 1.0, 0.0).astype(BF16)
    stats = jnp.dot(stats, spread, preferred_element_type=F32)
    peaks = stats[:, :HD].reshape(2, count, UNIT, HD)
    totals = stats[:, HD:].reshape(2, count, UNIT, HD)
    share = jnp.exp2(peaks - jnp.max(peaks, axis=(0, 1), keepdims=True))
    total = jnp.sum(totals * share, axis=(0, 1))
    accum = jnp.sum(mine[:, 2].astype(F32) * share[0], axis=0) + jnp.sum(other[:, 2].astype(F32) * share[1], axis=0)
    out[...] = (accum / total).astype(BF16)


def choose_kernel(span_list, span_slot, mine, other, near, far, out, held):
    core, hi = lax.axis_index("c"), lax.axis_index("hi")
    slots = out.shape[1] - 2
    held[0] = mine[:, 0:2]
    held[1] = other[:, 0:2]
    for p in range(out.shape[0]):
        for t in range(slots):
            block = span_slot[span_list[p, 2 * t + core]]
            source = ((block >> 5) << 3) | ((block >> 1) & 7)
            out[p, t] = held[((block >> 4) & 1) ^ core, source, block & 1]
        out[p, slots + hi] = near[...]
        out[p, slots + 1 - hi] = far[...]


def begin(scores, values):
    peak = jnp.max(scores, axis=1, keepdims=True)
    weights = jnp.exp2(scores * COEF - peak * COEF)
    total = jnp.sum(weights, axis=1, keepdims=True)
    accum = jnp.dot(weights.astype(BF16), values, preferred_element_type=F32)
    return peak, total, accum


def extend(state, scores, values):
    high, total, accum = state
    peak = jnp.maximum(high, jnp.max(scores, axis=1, keepdims=True))
    shrink = jnp.exp2((high - peak) * COEF)
    weights = jnp.exp2(scores * COEF - peak * COEF)
    total = total * shrink + jnp.sum(weights, axis=1, keepdims=True)
    accum = accum * shrink + jnp.dot(weights.astype(BF16), values, preferred_element_type=F32)
    return peak, total, accum


PART = 4


def doc_rows(ref, kind, first):
    parts = [ref[2 * y + kind, pl.ds(first, PART)].reshape(PART * UNIT, HD) for y in range(4)]
    return jnp.concatenate(parts, axis=0)


def over_documents(queries, state, count, own, other):
    core = lax.axis_index("c")
    slots = own.shape[1] - 2
    col = iota((1, 8 * PART * UNIT), 1)
    parity = core ^ (col // (4 * PART * UNIT))
    turn = (col // UNIT) & (PART - 1)

    def one(i, state):
        first = jnp.minimum(PART * i, slots - PART)
        keys = jnp.concatenate([doc_rows(own, 0, first), doc_rows(other, 0, first)], axis=0)
        values = jnp.concatenate([doc_rows(own, 1, first), doc_rows(other, 1, first)], axis=0)
        at = first + turn
        bias = jnp.where((at >= PART * i) & (2 * at + parity < count), 0.0, NEG)
        return extend(state, scores_of(queries, keys) + bias, values)

    return lax.fori_loop(0, (count + 2 * PART - 1) // (2 * PART), one, state)


def queries_of(q, far):
    wide = GROUP * HD
    if far:
        heads = [q[:, g * HD : (g + 1) * HD] for g in range(GROUP)]
    else:
        base = lax.axis_index("hi") * wide
        heads = [q[0, :, pl.ds(pl.multiple_of(base + g * HD, HD), HD)] for g in range(GROUP)]
    return jnp.concatenate(heads, axis=0)


def first_kernel(counts, lengths, q, p0, p1, p2, p3, a, b, stats, sums, *, far):
    hi, lo, core = lax.axis_index("hi"), lax.axis_index("lo"), lax.axis_index("c")
    lane = lane_of_decode()
    count, length = counts[lane], lengths[lane]
    rows = sums.shape[0]
    tok = rows // GROUP
    col = iota((1, 8 * tok), 1)
    kpos = ((core ^ (col >> 8)) << 6) | ((lo ^ ((col >> 7) & 1)) << 7) | ((hi ^ ((col >> 6) & 1)) << 8) | (col & 63)
    row = iota((rows, 1), 0)
    pkeys = jnp.concatenate([x[0].reshape(2 * tok, HD) for x in (p0, p1, p2, p3)], axis=0)
    pvalues = jnp.concatenate([x[1].reshape(2 * tok, HD) for x in (p0, p1, p2, p3)], axis=0)
    queries = queries_of(q, far)
    qpos = (((hi ^ far) << 2) | (lo << 1) | core) * tok + (row & (tok - 1))
    keep = (kpos <= qpos) & (kpos < length)
    state = begin(jnp.where(keep, scores_of(queries, pkeys), NEG), pvalues)
    peak, total, accum = over_documents(queries, state, count, a, b)
    sums[...] = accum
    stats[0] = jnp.broadcast_to(peak, sums.shape)
    stats[1] = jnp.broadcast_to(total, sums.shape)


def last_kernel(counts, q, c, d, stats, sums, out, *, far):
    count = counts[lane_of_decode()]
    tok = out.shape[0]
    queries = queries_of(q, far)
    peak = jnp.max(stats[0], axis=1, keepdims=True)
    total = jnp.max(stats[1], axis=1, keepdims=True)
    state = (peak, total, sums[...])
    _, total, accum = over_documents(queries, state, count, c, d)
    result = (accum / total).astype(out.dtype)
    for g in range(GROUP):
        out[:, g * HD : (g + 1) * HD] = result[g * tok : (g + 1) * tok]


def project_kernel(own, swapped, w, out, held):
    lo, mine = lax.axis_index("lo"), lax.axis_index("x")

    def rows(x):
        return jnp.concatenate([x[g, head] for head in range(2) for g in range(GROUP)], axis=1)

    terms = jnp.dot(jnp.concatenate([rows(own), rows(swapped)], axis=0), w[...], preferred_element_type=F32)
    held[pl.ds(pl.multiple_of(lo * UNIT, UNIT), UNIT)] = terms[:UNIT]
    held[pl.ds(pl.multiple_of((1 - lo) * UNIT, UNIT), UNIT)] = terms[UNIT:]
    piece = out.shape[1]
    for k in range(4):
        out[k] = held[pl.ds(pl.multiple_of((mine ^ k) * piece, piece), piece)]


def on_device(
    prompt_q,
    prompt_k,
    prompt_v,
    span_k,
    span_v,
    k_scale,
    v_scale,
    span_list,
    span_slot,
    span_count,
    prompt_len,
    decode_q,
    new_k,
    new_v,
    w_out,
):
    hi = lax.axis_index("hi")
    tok = prompt_q.shape[1]
    prompts, steps = decode_q.shape[:2]
    slots = span_list.shape[1]
    wide = GROUP * HD
    shape = jax.ShapeDtypeStruct

    payload = single(
        spread_kernel,
        shape((2, 2, 8, 4, UNIT, HD), BF16),
        2,
        5,
        (
            span_count,
            prompt_len,
            k_scale,
            v_scale,
            span_k,
            span_v,
            prompt_k,
            prompt_v,
            span_list,
            span_slot.reshape(1, -1),
            decode_q,
            new_k,
            new_v,
        ),
        [pltpu.VMEM((2, HD, 2 * HD), F32), pltpu.VMEM((prompts * steps, decode_q.shape[2]), F32)],
        limit=60,
    )
    mine = lax.all_to_all(payload.reshape(32, 4, UNIT, HD), RANKS, 0, 0, tiled=True)
    bundle = single(pack_kernel, shape((tok, wide + 2 * HD), BF16), 0, 1.5, (prompt_q, prompt_k, prompt_v), limit=60)
    mine, bundle = lax.optimization_barrier((mine, bundle))
    bundle = lax.ppermute(bundle, "hi", SWAP)
    other = lax.ppermute(mine, "c", SWAP)

    done = call(combine_kernel, shape((UNIT, HD), BF16), [VMEM] * 2, 1, mine, other)
    chosen = pl.pallas_call(
        choose_kernel,
        out_shape=shape((prompts, slots // 2 + 2, UNIT, HD), BF16),
        in_specs=[SMEM] * 2 + [VMEM] * 4,
        out_specs=VMEM,
        scratch_shapes=[pltpu.VMEM((2, 32, 2, UNIT, HD), BF16)],
        compiler_params=params(),
        cost_estimate=cost(1),
    )(span_list, span_slot, mine, other, done, lax.ppermute(done, "hi", SWAP))
    chosen, bundle = lax.optimization_barrier((chosen, bundle))
    p0 = single(pair_kernel, shape((2, 2, tok, HD), BF16), 0, 1.5, (prompt_k, prompt_v, bundle))
    p1 = lax.ppermute(p0, "lo", SWAP)
    p2 = lax.ppermute(p0, "c", SWAP)
    p3 = lax.ppermute(p1, "c", SWAP)
    a = lax.all_to_all(chosen, DECODE, 0, 0, tiled=True)
    a, p1, p2, p3 = lax.optimization_barrier((a, p1, p2, p3))
    c = lax.ppermute(a, "lo", SWAP)
    b = lax.ppermute(a, "c", SWAP)

    def first(queries, is_far):
        return pl.pallas_call(
            lambda *refs: first_kernel(*refs, far=is_far),
            out_shape=(shape((2, GROUP * tok, HD), F32), shape((GROUP * tok, HD), F32)),
            in_specs=[SMEM] * 2 + [VMEM] * 7,
            out_specs=(VMEM, VMEM),
            compiler_params=params(),
            cost_estimate=cost(4),
        )(span_count, prompt_len, queries, p0, p1, p2, p3, a, b)

    def last(queries, is_far, dtype, state):
        return call(
            lambda *refs: last_kernel(*refs, far=is_far),
            shape((tok, wide), dtype),
            [SMEM] + [VMEM] * 5,
            4,
            span_count,
            queries,
            c,
            d,
            *state,
        )

    far_state, near_state = first(bundle, 1), first(prompt_q, 0)
    c, far_state, near_state = lax.optimization_barrier((c, far_state, near_state))
    d = lax.ppermute(c, "c", SWAP)

    lanes = a.shape[0]
    last_units = pl.BlockSpec((lanes, 2, UNIT, HD), lambda i: (0, slots // 4, 0, 0))
    terms = pl.pallas_call(
        project_kernel,
        out_shape=shape((4, prompts * steps // 4, w_out.shape[1]), F32),
        grid=(1,),
        in_specs=[last_units] * 2 + [whole(w_out)],
        out_specs=pl.BlockSpec((4, prompts * steps // 4, w_out.shape[1]), lambda i: (0, 0, 0)),
        scratch_shapes=[pltpu.VMEM((prompts * steps, w_out.shape[1]), F32)],
        compiler_params=params(),
        cost_estimate=cost(1),
    )(a, c, w_out)
    given = lax.ppermute(jnp.stack([terms[1], terms[3]]), "x", [(i, i ^ 1) for i in range(4)])
    far_out = last(bundle, 1, BF16, far_state)
    prompt_q, far_out, terms, given = lax.optimization_barrier((prompt_q, far_out, terms, given))
    far_out = lax.ppermute(far_out, "hi", SWAP)
    near_out = last(prompt_q, 0, F32, near_state)
    near_out, summed = lax.optimization_barrier((near_out, terms[2] + given[1]))
    rest = lax.ppermute(summed, "x", [(i, i ^ 2) for i in range(4)])
    far_out = far_out.astype(F32)
    low = hi == 0
    prefill_out = jnp.concatenate(
        [jnp.where(low, near_out, far_out), jnp.where(low, far_out, near_out)], axis=1
    )[None]
    prefill_out, rest = lax.optimization_barrier((prefill_out, rest))
    decode_out = (terms[0] + given[0] + rest).astype(BF16)
    return prefill_out, decode_out


def solution(mesh):
    fine = Mesh(mesh.devices.reshape(2, 2, 2, 4, 4, 2), ("hi", "lo", "c", "x", "y", "zh"))
    store = ("hi", "lo", "c")
    owners = store + DECODE
    placed = (
        P(DECODE, store, "x"),
        P(DECODE, store, "x"),
        P(DECODE, store, "x"),
        P(owners, None, "x"),
        P(owners, None, "x"),
        P(owners, "x"),
        P(owners, "x"),
        P(),
        P(),
        P(),
        P(),
        P(None, None, "x"),
        P(None, None, "x"),
        P(None, None, "x"),
        P("x", owners),
    )
    return jax.shard_map(
        on_device,
        mesh=fine,
        in_specs=placed,
        out_specs=(P(DECODE, store, "x"), P("x", owners)),
        check_vma=False,
    )
```

```python
import math

import jax
import jax.numpy as jnp
from jax import lax
from jax.experimental import pallas as pl
from jax.experimental.pallas import tpu as pltpu
from jax.sharding import Mesh, PartitionSpec as P

NEG = -1e30
HD = 128
GROUP = 8
UNIT = 16
VMEM = pl.BlockSpec(memory_space=pltpu.VMEM)
SMEM = pl.BlockSpec(memory_space=pltpu.SMEM)
RANKS = ("hi", "lo", "y", "zh")
DECODE = ("y", "zh")
SWAP = [(0, 1), (1, 0)]
COEF = math.log2(math.e) / math.sqrt(HD)
BF16 = jnp.bfloat16
F32 = jnp.float32


def params(limit=40):
    return pltpu.CompilerParams(vmem_limit_bytes=limit << 20)


def cost(us):
    return pl.CostEstimate(flops=int(us * 1.1e9), bytes_accessed=1 << 16, transcendentals=0)


def call(kernel, out_shape, in_specs, us, *args):
    return pl.pallas_call(
        kernel,
        out_shape=out_shape,
        in_specs=in_specs,
        out_specs=VMEM,
        compiler_params=params(),
        cost_estimate=cost(us),
    )(*args)


def whole(x):
    return pl.BlockSpec(x.shape, lambda i: (0,) * len(x.shape))


def single(kernel, out, scalars, us, args, scratch=(), limit=40):
    return pl.pallas_call(
        kernel,
        grid=(1,),
        out_shape=out,
        in_specs=[SMEM] * scalars + [whole(x) for x in args[scalars:]],
        out_specs=whole(out),
        scratch_shapes=list(scratch),
        compiler_params=params(limit),
        cost_estimate=cost(us),
    )(*args)


def lane_of_decode():
    return lax.axis_index("y") * 2 + lax.axis_index("zh")


def scores_of(queries, keys):
    return lax.dot_general(queries, keys, (((1,), (1,)), ((), ())), preferred_element_type=F32)


def iota(shape, dim):
    return lax.broadcasted_iota(jnp.int32, shape, dim)


def pack_kernel(q, out):
    wide = GROUP * HD
    out[...] = q[0, :, pl.ds(pl.multiple_of((1 - lax.axis_index("hi")) * wide, wide), wide)]


def pack_keys_kernel(k, v, out):
    at = pl.ds(pl.multiple_of((1 - lax.axis_index("hi")) * HD, HD), HD)
    out[0] = k[0, :, at]
    out[1] = v[0, :, at]


def pair_kernel(k, v, bundle, out):
    at = pl.ds(pl.multiple_of(lax.axis_index("hi") * HD, HD), HD)
    out[0, 0] = k[0, :, at]
    out[1, 0] = v[0, :, at]
    out[0, 1] = bundle[0]
    out[1, 1] = bundle[1]


def spread_kernel(
    counts, lengths, k_scale, v_scale, span_k, span_v, prompt_k, prompt_v, span_list, span_slot, decode_q, new_k, new_v, out, fresh, dq
):
    tok = prompt_k.shape[1]
    prompts, steps = new_k.shape[:2]
    rows = prompts * steps
    lane = lane_of_decode()
    place = lax.axis_index("hi") * 4 + lax.axis_index("lo") * 2 + lax.axis_index("c")
    keys, values = [], []
    for kind, (codes, scale, full) in enumerate(((span_k, k_scale, keys), (span_v, v_scale, values))):
        factors = scale[...].astype(F32)
        for head in range(2):
            full.append([])
            for block in range(2):
                part = codes[block, :, head * HD : (head + 1) * HD].astype(F32)
                part = (part * factors[block : block + 1, head : head + 1]).astype(BF16)
                full[head].append(part)
                units = part.reshape(2, 4, UNIT, HD)
                for half in range(2):
                    for y in range(4):
                        out[head, half, 2 * y + kind, block] = units[half, y]
    for p in range(prompts):
        dq[p * steps : (p + 1) * steps] = decode_q[p].astype(F32)
    fresh[...] = jnp.zeros_like(fresh)
    fresh[0, 0:steps] = new_k[lane].astype(F32)
    fresh[1, 0:steps] = new_v[lane].astype(F32)
    width = 4 * HD
    row = iota((rows, 1), 0)
    prompt = row // steps
    step = row % steps
    listed = jnp.zeros((rows, span_list.shape[1]), jnp.int32)
    used = jnp.zeros((rows, 1), jnp.int32)
    for p in range(prompts):
        listed = jnp.where(prompt == p, span_list[p : p + 1, :], listed)
        used = jnp.where(prompt == p, counts[p], used)
    live = iota(listed.shape, 1) < used
    col = iota((rows, width), 1)
    slot = span_slot[...]
    first = (place * prompts + lane) * 2
    keep = jnp.zeros((rows, width), jnp.int32)
    for block in range(2):
        name = jnp.sum(jnp.where(slot == first + block, iota(slot.shape, 1), 0), axis=1, keepdims=True)
        has = jnp.max(jnp.where(live & (listed == name), 1, 0), axis=1, keepdims=True)
        keep = jnp.where((col >> 7) == block, has, keep)
    mine = jnp.where(prompt == lane, 1, 0)
    at = col - 2 * HD
    old = jnp.where((at >= 0) & (at < tok) & (place * tok + at < lengths[lane]), 1, 0)
    new = jnp.where((at >= HD) & (at - HD <= step) & (place == 0), 1, 0)
    keep = jnp.where(at >= 0, (old | new) * mine, keep)
    keep = (keep > 0)[None]
    for head in range(2):
        lanes = slice(head * HD, (head + 1) * HD)
        gap = jnp.zeros((HD - tok, HD), BF16)
        k_all = jnp.concatenate(keys[head] + [prompt_k[0, :, lanes], gap, fresh[0, :, lanes].astype(BF16)], axis=0)
        v_all = jnp.concatenate(values[head] + [prompt_v[0, :, lanes], gap, fresh[1, :, lanes].astype(BF16)], axis=0)
        base = head * GROUP
        queries = jnp.concatenate([dq[:, (base + g) * HD : (base + g + 1) * HD] for g in range(GROUP)], axis=0).astype(BF16)
        scores = scores_of(queries, k_all).reshape(GROUP, rows, width)
        scores = jnp.where(keep, scores, NEG) * COEF
        peak = jnp.max(scores, axis=2, keepdims=True)
        peak_hi = peak.astype(BF16).astype(F32)
        peak_lo = (peak - peak_hi).astype(BF16).astype(F32)
        weights = jnp.where(keep, jnp.exp2(scores - (peak_hi + peak_lo)), 0.0)
        total = jnp.sum(weights, axis=2, keepdims=True)
        total_hi = total.astype(BF16).astype(F32)
        total_lo = total - total_hi
        accum = jnp.dot(weights.reshape(GROUP * rows, width).astype(BF16), v_all, preferred_element_type=F32)
        accum = accum.astype(BF16).reshape(GROUP, 2, UNIT, HD)
        at = iota((GROUP, rows, HD), 2)
        stats = jnp.where(at == 0, peak_hi, jnp.where(at == 1, peak_lo, jnp.where(at == 2, total_hi, total_lo)))
        stats = jnp.where(at < 4, stats, 0.0).astype(BF16).reshape(GROUP, 2, UNIT, HD)
        for half in range(2):
            out[head, half, :, 2] = accum[:, half]
            out[head, half, :, 3] = stats[:, half]


def combine_kernel(mine, other, out):
    count = mine.shape[0]
    stats = jnp.concatenate([x[:, 3].reshape(count * UNIT, HD) for x in (mine, other)], axis=0)
    row, col = iota((HD, 2 * HD), 0), iota((HD, 2 * HD), 1)
    spread = jnp.where((row < 4) & ((row >> 1) == (col >> 7)), 1.0, 0.0).astype(BF16)
    stats = jnp.dot(stats, spread, preferred_element_type=F32)
    peaks = stats[:, :HD].reshape(2, count, UNIT, HD)
    totals = stats[:, HD:].reshape(2, count, UNIT, HD)
    share = jnp.exp2(peaks - jnp.max(peaks, axis=(0, 1), keepdims=True))
    total = jnp.sum(totals * share, axis=(0, 1))
    accum = jnp.sum(mine[:, 2].astype(F32) * share[0], axis=0) + jnp.sum(other[:, 2].astype(F32) * share[1], axis=0)
    out[...] = (accum / total).astype(BF16)


def choose_kernel(span_list, span_slot, mine, other, near, far, out, held):
    core, hi = lax.axis_index("c"), lax.axis_index("hi")
    slots = out.shape[1] - 2
    held[0] = mine[:, 0:2]
    held[1] = other[:, 0:2]
    for p in range(out.shape[0]):
        for t in range(slots):
            block = span_slot[span_list[p, 2 * t + core]]
            source = ((block >> 5) << 3) | ((block >> 1) & 7)
            out[p, t] = held[((block >> 4) & 1) ^ core, source, block & 1]
        out[p, slots + hi] = near[...]
        out[p, slots + 1 - hi] = far[...]


def begin(scores, values):
    peak = jnp.max(scores, axis=1, keepdims=True)
    weights = jnp.exp2(scores * COEF - peak * COEF)
    total = jnp.sum(weights, axis=1, keepdims=True)
    accum = jnp.dot(weights.astype(BF16), values, preferred_element_type=F32)
    return peak, total, accum


def extend(state, scores, values):
    high, total, accum = state
    peak = jnp.maximum(high, jnp.max(scores, axis=1, keepdims=True))
    shrink = jnp.exp2((high - peak) * COEF)
    weights = jnp.exp2(scores * COEF - peak * COEF)
    total = total * shrink + jnp.sum(weights, axis=1, keepdims=True)
    accum = accum * shrink + jnp.dot(weights.astype(BF16), values, preferred_element_type=F32)
    return peak, total, accum


PART = 4


def doc_rows(ref, kind, first):
    parts = [ref[2 * y + kind, pl.ds(first, PART)].reshape(PART * UNIT, HD) for y in range(4)]
    return jnp.concatenate(parts, axis=0)


def over_documents(queries, state, count, own, other):
    core = lax.axis_index("c")
    slots = own.shape[1] - 2
    col = iota((1, 8 * PART * UNIT), 1)
    parity = core ^ (col // (4 * PART * UNIT))
    turn = (col // UNIT) & (PART - 1)

    def one(i, state):
        first = jnp.minimum(PART * i, slots - PART)
        keys = jnp.concatenate([doc_rows(own, 0, first), doc_rows(other, 0, first)], axis=0)
        values = jnp.concatenate([doc_rows(own, 1, first), doc_rows(other, 1, first)], axis=0)
        at = first + turn
        bias = jnp.where((at >= PART * i) & (2 * at + parity < count), 0.0, NEG)
        return extend(state, scores_of(queries, keys) + bias, values)

    return lax.fori_loop(0, (count + 2 * PART - 1) // (2 * PART), one, state)


def queries_of(q, far):
    wide = GROUP * HD
    if far:
        heads = [q[:, g * HD : (g + 1) * HD] for g in range(GROUP)]
    else:
        base = lax.axis_index("hi") * wide
        heads = [q[0, :, pl.ds(pl.multiple_of(base + g * HD, HD), HD)] for g in range(GROUP)]
    return jnp.concatenate(heads, axis=0)


def first_kernel(counts, lengths, q, p0, p1, p2, p3, a, b, stats, sums, *, far):
    hi, lo, core = lax.axis_index("hi"), lax.axis_index("lo"), lax.axis_index("c")
    lane = lane_of_decode()
    count, length = counts[lane], lengths[lane]
    rows = sums.shape[0]
    tok = rows // GROUP
    col = iota((1, 8 * tok), 1)
    kpos = ((core ^ (col >> 8)) << 6) | ((lo ^ ((col >> 7) & 1)) << 7) | ((hi ^ ((col >> 6) & 1)) << 8) | (col & 63)
    row = iota((rows, 1), 0)
    pkeys = jnp.concatenate([x[0].reshape(2 * tok, HD) for x in (p0, p1, p2, p3)], axis=0)
    pvalues = jnp.concatenate([x[1].reshape(2 * tok, HD) for x in (p0, p1, p2, p3)], axis=0)
    queries = queries_of(q, far)
    qpos = (((hi ^ far) << 2) | (lo << 1) | core) * tok + (row & (tok - 1))
    keep = (kpos <= qpos) & (kpos < length)
    state = begin(jnp.where(keep, scores_of(queries, pkeys), NEG), pvalues)
    peak, total, accum = over_documents(queries, state, count, a, b)
    sums[...] = accum
    stats[0] = jnp.broadcast_to(peak, sums.shape)
    stats[1] = jnp.broadcast_to(total, sums.shape)


def last_kernel(counts, q, c, d, stats, sums, out, *, far):
    count = counts[lane_of_decode()]
    tok = out.shape[0]
    queries = queries_of(q, far)
    peak = jnp.max(stats[0], axis=1, keepdims=True)
    total = jnp.max(stats[1], axis=1, keepdims=True)
    state = (peak, total, sums[...])
    _, total, accum = over_documents(queries, state, count, c, d)
    result = (accum / total).astype(out.dtype)
    for g in range(GROUP):
        out[:, g * HD : (g + 1) * HD] = result[g * tok : (g + 1) * tok]


def project_kernel(own, swapped, w, out, held):
    lo, mine = lax.axis_index("lo"), lax.axis_index("x")

    def rows(x):
        return jnp.concatenate([x[g, head] for head in range(2) for g in range(GROUP)], axis=1)

    terms = jnp.dot(jnp.concatenate([rows(own), rows(swapped)], axis=0), w[...], preferred_element_type=F32)
    held[pl.ds(pl.multiple_of(lo * UNIT, UNIT), UNIT)] = terms[:UNIT]
    held[pl.ds(pl.multiple_of((1 - lo) * UNIT, UNIT), UNIT)] = terms[UNIT:]
    piece = out.shape[1]
    for k in range(4):
        out[k] = held[pl.ds(pl.multiple_of((mine ^ k) * piece, piece), piece)]


def on_device(
    prompt_q,
    prompt_k,
    prompt_v,
    span_k,
    span_v,
    k_scale,
    v_scale,
    span_list,
    span_slot,
    span_count,
    prompt_len,
    decode_q,
    new_k,
    new_v,
    w_out,
):
    hi = lax.axis_index("hi")
    tok = prompt_q.shape[1]
    prompts, steps = decode_q.shape[:2]
    slots = span_list.shape[1]
    wide = GROUP * HD
    shape = jax.ShapeDtypeStruct

    payload = single(
        spread_kernel,
        shape((2, 2, 8, 4, UNIT, HD), BF16),
        2,
        5,
        (
            span_count,
            prompt_len,
            k_scale,
            v_scale,
            span_k,
            span_v,
            prompt_k,
            prompt_v,
            span_list,
            span_slot.reshape(1, -1),
            decode_q,
            new_k,
            new_v,
        ),
        [pltpu.VMEM((2, HD, 2 * HD), F32), pltpu.VMEM((prompts * steps, decode_q.shape[2]), F32)],
        limit=60,
    )
    mine = lax.all_to_all(payload.reshape(32, 4, UNIT, HD), RANKS, 0, 0, tiled=True)
    bundle = single(pack_kernel, shape((tok, wide), BF16), 0, 1.5, (prompt_q,), limit=60)
    pairs = single(pack_keys_kernel, shape((2, tok, HD), BF16), 0, 1, (prompt_k, prompt_v), limit=60)
    mine, bundle, pairs = lax.optimization_barrier((mine, bundle, pairs))
    pairs = lax.ppermute(pairs, "hi", SWAP)
    bundle = lax.ppermute(bundle, "hi", SWAP)
    other = lax.ppermute(mine, "c", SWAP)

    done = call(combine_kernel, shape((UNIT, HD), BF16), [VMEM] * 2, 1, mine, other)
    chosen = pl.pallas_call(
        choose_kernel,
        out_shape=shape((prompts, slots // 2 + 2, UNIT, HD), BF16),
        in_specs=[SMEM] * 2 + [VMEM] * 4,
        out_specs=VMEM,
        scratch_shapes=[pltpu.VMEM((2, 32, 2, UNIT, HD), BF16)],
        compiler_params=params(),
        cost_estimate=cost(1),
    )(span_list, span_slot, mine, other, done, lax.ppermute(done, "hi", SWAP))
    chosen, pairs = lax.optimization_barrier((chosen, pairs))
    p0 = single(pair_kernel, shape((2, 2, tok, HD), BF16), 0, 1.5, (prompt_k, prompt_v, pairs))
    p1 = lax.ppermute(p0, "lo", SWAP)
    p2 = lax.ppermute(p0, "c", SWAP)
    p3 = lax.ppermute(p1, "c", SWAP)
    a = lax.all_to_all(chosen, DECODE, 0, 0, tiled=True)
    a, p1, p2, p3, bundle = lax.optimization_barrier((a, p1, p2, p3, bundle))
    c = lax.ppermute(a, "lo", SWAP)
    b = lax.ppermute(a, "c", SWAP)

    def first(queries, is_far):
        return pl.pallas_call(
            lambda *refs: first_kernel(*refs, far=is_far),
            out_shape=(shape((2, GROUP * tok, HD), F32), shape((GROUP * tok, HD), F32)),
            in_specs=[SMEM] * 2 + [VMEM] * 7,
            out_specs=(VMEM, VMEM),
            compiler_params=params(),
            cost_estimate=cost(4),
        )(span_count, prompt_len, queries, p0, p1, p2, p3, a, b)

    def last(queries, is_far, dtype, state):
        return call(
            lambda *refs: last_kernel(*refs, far=is_far),
            shape((tok, wide), dtype),
            [SMEM] + [VMEM] * 5,
            4,
            span_count,
            queries,
            c,
            d,
            *state,
        )

    far_state, near_state = first(bundle, 1), first(prompt_q, 0)
    c, far_state, near_state = lax.optimization_barrier((c, far_state, near_state))
    d = lax.ppermute(c, "c", SWAP)

    lanes = a.shape[0]
    last_units = pl.BlockSpec((lanes, 2, UNIT, HD), lambda i: (0, slots // 4, 0, 0))
    terms = pl.pallas_call(
        project_kernel,
        out_shape=shape((4, prompts * steps // 4, w_out.shape[1]), F32),
        grid=(1,),
        in_specs=[last_units] * 2 + [whole(w_out)],
        out_specs=pl.BlockSpec((4, prompts * steps // 4, w_out.shape[1]), lambda i: (0, 0, 0)),
        scratch_shapes=[pltpu.VMEM((prompts * steps, w_out.shape[1]), F32)],
        compiler_params=params(),
        cost_estimate=cost(1),
    )(a, c, w_out)
    given = lax.ppermute(jnp.stack([terms[1], terms[3]]), "x", [(i, i ^ 1) for i in range(4)])
    far_out = last(bundle, 1, BF16, far_state)
    prompt_q, far_out, terms, given = lax.optimization_barrier((prompt_q, far_out, terms, given))
    far_out = lax.ppermute(far_out, "hi", SWAP)
    near_out = last(prompt_q, 0, F32, near_state)
    near_out, summed = lax.optimization_barrier((near_out, terms[2] + given[1]))
    rest = lax.ppermute(summed, "x", [(i, i ^ 2) for i in range(4)])
    far_out = far_out.astype(F32)
    low = hi == 0
    prefill_out = jnp.concatenate(
        [jnp.where(low, near_out, far_out), jnp.where(low, far_out, near_out)], axis=1
    )[None]
    prefill_out, rest = lax.optimization_barrier((prefill_out, rest))
    decode_out = (terms[0] + given[0] + rest).astype(BF16)
    return prefill_out, decode_out


def solution(mesh):
    fine = Mesh(mesh.devices.reshape(2, 2, 2, 4, 4, 2), ("hi", "lo", "c", "x", "y", "zh"))
    store = ("hi", "lo", "c")
    owners = store + DECODE
    placed = (
        P(DECODE, store, "x"),
        P(DECODE, store, "x"),
        P(DECODE, store, "x"),
        P(owners, None, "x"),
        P(owners, None, "x"),
        P(owners, "x"),
        P(owners, "x"),
        P(),
        P(),
        P(),
        P(),
        P(None, None, "x"),
        P(None, None, "x"),
        P(None, None, "x"),
        P("x", owners),
    )
    return jax.shard_map(
        on_device,
        mesh=fine,
        in_specs=placed,
        out_specs=(P(DECODE, store, "x"), P("x", owners)),
        check_vma=False,
    )
```

```python
import math

import jax
import jax.numpy as jnp
from jax import lax
from jax.experimental import pallas as pl
from jax.experimental.pallas import tpu as pltpu
from jax.sharding import Mesh, PartitionSpec as P

NEG = -1e30
HD = 128
GROUP = 8
UNIT = 16
VMEM = pl.BlockSpec(memory_space=pltpu.VMEM)
SMEM = pl.BlockSpec(memory_space=pltpu.SMEM)
RANKS = ("hi", "lo", "y", "zh")
DECODE = ("y", "zh")
SWAP = [(0, 1), (1, 0)]
COEF = math.log2(math.e) / math.sqrt(HD)
BF16 = jnp.bfloat16
F32 = jnp.float32


def params(limit=40):
    return pltpu.CompilerParams(vmem_limit_bytes=limit << 20)


def cost(us):
    return pl.CostEstimate(flops=int(us * 1.1e9), bytes_accessed=1 << 16, transcendentals=0)


def call(kernel, out_shape, in_specs, us, *args):
    return pl.pallas_call(
        kernel,
        out_shape=out_shape,
        in_specs=in_specs,
        out_specs=VMEM,
        compiler_params=params(),
        cost_estimate=cost(us),
    )(*args)


def whole(x):
    return pl.BlockSpec(x.shape, lambda i: (0,) * len(x.shape))


def single(kernel, out, scalars, us, args, scratch=(), limit=40):
    return pl.pallas_call(
        kernel,
        grid=(1,),
        out_shape=out,
        in_specs=[SMEM] * scalars + [whole(x) for x in args[scalars:]],
        out_specs=whole(out),
        scratch_shapes=list(scratch),
        compiler_params=params(limit),
        cost_estimate=cost(us),
    )(*args)


def lane_of_decode():
    return lax.axis_index("y") * 2 + lax.axis_index("zh")


def scores_of(queries, keys):
    return lax.dot_general(queries, keys, (((1,), (1,)), ((), ())), preferred_element_type=F32)


def iota(shape, dim):
    return lax.broadcasted_iota(jnp.int32, shape, dim)


def pack_kernel(q, out):
    wide = GROUP * HD
    out[...] = q[0, :, pl.ds(pl.multiple_of((1 - lax.axis_index("hi")) * wide, wide), wide)]


def pack_keys_kernel(k, v, out):
    at = pl.ds(pl.multiple_of((1 - lax.axis_index("hi")) * HD, HD), HD)
    out[0] = k[0, :, at]
    out[1] = v[0, :, at]


def pair_kernel(k, v, bundle, out):
    at = pl.ds(pl.multiple_of(lax.axis_index("hi") * HD, HD), HD)
    out[0, 0] = k[0, :, at]
    out[1, 0] = v[0, :, at]
    out[0, 1] = bundle[0]
    out[1, 1] = bundle[1]


def spread_kernel(
    counts, lengths, k_scale, v_scale, span_k, span_v, prompt_k, prompt_v, span_list, span_slot, decode_q, new_k, new_v, out, fresh, dq
):
    tok = prompt_k.shape[1]
    prompts, steps = new_k.shape[:2]
    rows = prompts * steps
    lane = lane_of_decode()
    place = lax.axis_index("hi") * 4 + lax.axis_index("lo") * 2 + lax.axis_index("c")
    keys, values = [], []
    for kind, (codes, scale, full) in enumerate(((span_k, k_scale, keys), (span_v, v_scale, values))):
        factors = scale[...].astype(F32)
        for head in range(2):
            full.append([])
            for block in range(2):
                part = codes[block, :, head * HD : (head + 1) * HD].astype(F32)
                part = (part * factors[block : block + 1, head : head + 1]).astype(BF16)
                full[head].append(part)
                units = part.reshape(2, 4, UNIT, HD)
                for half in range(2):
                    for y in range(4):
                        out[head, half, 2 * y + kind, block] = units[half, y]
    for p in range(prompts):
        dq[p * steps : (p + 1) * steps] = decode_q[p].astype(F32)
    fresh[...] = jnp.zeros_like(fresh)
    fresh[0, 0:steps] = new_k[lane].astype(F32)
    fresh[1, 0:steps] = new_v[lane].astype(F32)
    width = 4 * HD
    row = iota((rows, 1), 0)
    prompt = row // steps
    step = row % steps
    listed = jnp.zeros((rows, span_list.shape[1]), jnp.int32)
    used = jnp.zeros((rows, 1), jnp.int32)
    for p in range(prompts):
        listed = jnp.where(prompt == p, span_list[p : p + 1, :], listed)
        used = jnp.where(prompt == p, counts[p], used)
    live = iota(listed.shape, 1) < used
    col = iota((rows, width), 1)
    slot = span_slot[...]
    first = (place * prompts + lane) * 2
    keep = jnp.zeros((rows, width), jnp.int32)
    for block in range(2):
        name = jnp.sum(jnp.where(slot == first + block, iota(slot.shape, 1), 0), axis=1, keepdims=True)
        has = jnp.max(jnp.where(live & (listed == name), 1, 0), axis=1, keepdims=True)
        keep = jnp.where((col >> 7) == block, has, keep)
    mine = jnp.where(prompt == lane, 1, 0)
    at = col - 2 * HD
    old = jnp.where((at >= 0) & (at < tok) & (place * tok + at < lengths[lane]), 1, 0)
    new = jnp.where((at >= HD) & (at - HD <= step) & (place == 0), 1, 0)
    keep = jnp.where(at >= 0, (old | new) * mine, keep)
    keep = (keep > 0)[None]
    for head in range(2):
        lanes = slice(head * HD, (head + 1) * HD)
        gap = jnp.zeros((HD - tok, HD), BF16)
        k_all = jnp.concatenate(keys[head] + [prompt_k[0, :, lanes], gap, fresh[0, :, lanes].astype(BF16)], axis=0)
        v_all = jnp.concatenate(values[head] + [prompt_v[0, :, lanes], gap, fresh[1, :, lanes].astype(BF16)], axis=0)
        base = head * GROUP
        queries = jnp.concatenate([dq[:, (base + g) * HD : (base + g + 1) * HD] for g in range(GROUP)], axis=0).astype(BF16)
        scores = scores_of(queries, k_all).reshape(GROUP, rows, width)
        scores = jnp.where(keep, scores, NEG) * COEF
        peak = jnp.max(scores, axis=2, keepdims=True)
        peak_hi = peak.astype(BF16).astype(F32)
        peak_lo = (peak - peak_hi).astype(BF16).astype(F32)
        weights = jnp.where(keep, jnp.exp2(scores - (peak_hi + peak_lo)), 0.0)
        total = jnp.sum(weights, axis=2, keepdims=True)
        total_hi = total.astype(BF16).astype(F32)
        total_lo = total - total_hi
        accum = jnp.dot(weights.reshape(GROUP * rows, width).astype(BF16), v_all, preferred_element_type=F32)
        accum = accum.astype(BF16).reshape(GROUP, 2, UNIT, HD)
        at = iota((GROUP, rows, HD), 2)
        stats = jnp.where(at == 0, peak_hi, jnp.where(at == 1, peak_lo, jnp.where(at == 2, total_hi, total_lo)))
        stats = jnp.where(at < 4, stats, 0.0).astype(BF16).reshape(GROUP, 2, UNIT, HD)
        for half in range(2):
            out[head, half, :, 2] = accum[:, half]
            out[head, half, :, 3] = stats[:, half]


def combine_kernel(mine, other, out):
    count = mine.shape[0]
    stats = jnp.concatenate([x[:, 3].reshape(count * UNIT, HD) for x in (mine, other)], axis=0)
    row, col = iota((HD, 2 * HD), 0), iota((HD, 2 * HD), 1)
    spread = jnp.where((row < 4) & ((row >> 1) == (col >> 7)), 1.0, 0.0).astype(BF16)
    stats = jnp.dot(stats, spread, preferred_element_type=F32)
    peaks = stats[:, :HD].reshape(2, count, UNIT, HD)
    totals = stats[:, HD:].reshape(2, count, UNIT, HD)
    share = jnp.exp2(peaks - jnp.max(peaks, axis=(0, 1), keepdims=True))
    total = jnp.sum(totals * share, axis=(0, 1))
    accum = jnp.sum(mine[:, 2].astype(F32) * share[0], axis=0) + jnp.sum(other[:, 2].astype(F32) * share[1], axis=0)
    out[...] = (accum / total).astype(BF16)


def choose_kernel(span_list, span_slot, mine, other, near, far, out, held):
    core, hi = lax.axis_index("c"), lax.axis_index("hi")
    slots = out.shape[1] - 2
    held[0] = mine[:, 0:2]
    held[1] = other[:, 0:2]
    for p in range(out.shape[0]):
        for t in range(slots):
            block = span_slot[span_list[p, 2 * t + core]]
            source = ((block >> 5) << 3) | ((block >> 1) & 7)
            out[p, t] = held[((block >> 4) & 1) ^ core, source, block & 1]
        out[p, slots + hi] = near[...]
        out[p, slots + 1 - hi] = far[...]


def begin(scores, values):
    peak = jnp.max(scores, axis=1, keepdims=True)
    weights = jnp.exp2(scores * COEF - peak * COEF)
    total = jnp.sum(weights, axis=1, keepdims=True)
    accum = jnp.dot(weights.astype(BF16), values, preferred_element_type=F32)
    return peak, total, accum


def extend(state, scores, values):
    high, total, accum = state
    peak = jnp.maximum(high, jnp.max(scores, axis=1, keepdims=True))
    shrink = jnp.exp2((high - peak) * COEF)
    weights = jnp.exp2(scores * COEF - peak * COEF)
    total = total * shrink + jnp.sum(weights, axis=1, keepdims=True)
    accum = accum * shrink + jnp.dot(weights.astype(BF16), values, preferred_element_type=F32)
    return peak, total, accum


PART = 4


def doc_rows(ref, kind, first):
    parts = [ref[2 * y + kind, pl.ds(first, PART)].reshape(PART * UNIT, HD) for y in range(4)]
    return jnp.concatenate(parts, axis=0)


def over_documents(queries, state, count, own, other):
    core = lax.axis_index("c")
    slots = own.shape[1] - 2
    col = iota((1, 8 * PART * UNIT), 1)
    parity = core ^ (col // (4 * PART * UNIT))
    turn = (col // UNIT) & (PART - 1)

    def one(i, state):
        first = jnp.minimum(PART * i, slots - PART)
        keys = jnp.concatenate([doc_rows(own, 0, first), doc_rows(other, 0, first)], axis=0)
        values = jnp.concatenate([doc_rows(own, 1, first), doc_rows(other, 1, first)], axis=0)
        at = first + turn
        bias = jnp.where((at >= PART * i) & (2 * at + parity < count), 0.0, NEG)
        return extend(state, scores_of(queries, keys) + bias, values)

    return lax.fori_loop(0, (count + 2 * PART - 1) // (2 * PART), one, state)


def queries_of(q, far):
    wide = GROUP * HD
    if far:
        heads = [q[:, g * HD : (g + 1) * HD] for g in range(GROUP)]
    else:
        base = lax.axis_index("hi") * wide
        heads = [q[0, :, pl.ds(pl.multiple_of(base + g * HD, HD), HD)] for g in range(GROUP)]
    return jnp.concatenate(heads, axis=0)


def first_kernel(counts, lengths, q, p0, p1, p2, p3, a, b, stats, sums, *, far):
    hi, lo, core = lax.axis_index("hi"), lax.axis_index("lo"), lax.axis_index("c")
    lane = lane_of_decode()
    count, length = counts[lane], lengths[lane]
    rows = sums.shape[0]
    tok = rows // GROUP
    col = iota((1, 8 * tok), 1)
    kpos = ((core ^ (col >> 8)) << 6) | ((lo ^ ((col >> 7) & 1)) << 7) | ((hi ^ ((col >> 6) & 1)) << 8) | (col & 63)
    row = iota((rows, 1), 0)
    pkeys = jnp.concatenate([x[0].reshape(2 * tok, HD) for x in (p0, p1, p2, p3)], axis=0)
    pvalues = jnp.concatenate([x[1].reshape(2 * tok, HD) for x in (p0, p1, p2, p3)], axis=0)
    queries = queries_of(q, far)
    qpos = (((hi ^ far) << 2) | (lo << 1) | core) * tok + (row & (tok - 1))
    keep = (kpos <= qpos) & (kpos < length)
    state = begin(jnp.where(keep, scores_of(queries, pkeys), NEG), pvalues)
    peak, total, accum = over_documents(queries, state, count, a, b)
    sums[...] = accum
    stats[0] = jnp.broadcast_to(peak, sums.shape)
    stats[1] = jnp.broadcast_to(total, sums.shape)


def last_kernel(counts, q, c, d, stats, sums, out, *, far):
    count = counts[lane_of_decode()]
    tok = out.shape[0]
    queries = queries_of(q, far)
    peak = jnp.max(stats[0], axis=1, keepdims=True)
    total = jnp.max(stats[1], axis=1, keepdims=True)
    state = (peak, total, sums[...])
    _, total, accum = over_documents(queries, state, count, c, d)
    result = (accum / total).astype(out.dtype)
    for g in range(GROUP):
        out[:, g * HD : (g + 1) * HD] = result[g * tok : (g + 1) * tok]


def project_kernel(own, swapped, w, out, held):
    lo, mine = lax.axis_index("lo"), lax.axis_index("x")

    def rows(x):
        return jnp.concatenate([x[g, head] for head in range(2) for g in range(GROUP)], axis=1)

    terms = jnp.dot(jnp.concatenate([rows(own), rows(swapped)], axis=0), w[...], preferred_element_type=F32)
    held[pl.ds(pl.multiple_of(lo * UNIT, UNIT), UNIT)] = terms[:UNIT]
    held[pl.ds(pl.multiple_of((1 - lo) * UNIT, UNIT), UNIT)] = terms[UNIT:]
    piece = out.shape[1]
    for k in range(4):
        out[k] = held[pl.ds(pl.multiple_of((mine ^ k) * piece, piece), piece)]


def on_device(
    prompt_q,
    prompt_k,
    prompt_v,
    span_k,
    span_v,
    k_scale,
    v_scale,
    span_list,
    span_slot,
    span_count,
    prompt_len,
    decode_q,
    new_k,
    new_v,
    w_out,
):
    hi = lax.axis_index("hi")
    tok = prompt_q.shape[1]
    prompts, steps = decode_q.shape[:2]
    slots = span_list.shape[1]
    wide = GROUP * HD
    shape = jax.ShapeDtypeStruct

    payload = single(
        spread_kernel,
        shape((2, 2, 8, 4, UNIT, HD), BF16),
        2,
        5,
        (
            span_count,
            prompt_len,
            k_scale,
            v_scale,
            span_k,
            span_v,
            prompt_k,
            prompt_v,
            span_list,
            span_slot.reshape(1, -1),
            decode_q,
            new_k,
            new_v,
        ),
        [pltpu.VMEM((2, HD, 2 * HD), F32), pltpu.VMEM((prompts * steps, decode_q.shape[2]), F32)],
        limit=60,
    )
    mine = lax.all_to_all(payload.reshape(32, 4, UNIT, HD), RANKS, 0, 0, tiled=True)
    bundle = single(pack_kernel, shape((tok, wide), BF16), 0, 1.5, (prompt_q,), limit=60)
    pairs = single(pack_keys_kernel, shape((2, tok, HD), BF16), 0, 1, (prompt_k, prompt_v), limit=60)
    mine, bundle, pairs = lax.optimization_barrier((mine, bundle, pairs))
    pairs = lax.ppermute(pairs, "hi", SWAP)
    bundle = lax.ppermute(bundle, "hi", SWAP)
    other = lax.ppermute(mine, "c", SWAP)

    done = call(combine_kernel, shape((UNIT, HD), BF16), [VMEM] * 2, 1, mine, other)
    chosen = pl.pallas_call(
        choose_kernel,
        out_shape=shape((prompts, slots // 2 + 2, UNIT, HD), BF16),
        in_specs=[SMEM] * 2 + [VMEM] * 4,
        out_specs=VMEM,
        scratch_shapes=[pltpu.VMEM((2, 32, 2, UNIT, HD), BF16)],
        compiler_params=params(),
        cost_estimate=cost(1),
    )(span_list, span_slot, mine, other, done, lax.ppermute(done, "hi", SWAP))
    chosen, pairs = lax.optimization_barrier((chosen, pairs))
    p0 = single(pair_kernel, shape((2, 2, tok, HD), BF16), 0, 1.5, (prompt_k, prompt_v, pairs))
    p1 = lax.ppermute(p0, "lo", SWAP)
    p2 = lax.ppermute(p0, "c", SWAP)
    p3 = lax.ppermute(p1, "c", SWAP)
    a = lax.all_to_all(chosen, DECODE, 0, 0, tiled=True)
    a, p1, p2, p3, bundle = lax.optimization_barrier((a, p1, p2, p3, bundle))
    c = lax.ppermute(a, "lo", SWAP)
    b = lax.ppermute(a, "c", SWAP)

    def first(queries, is_far):
        return pl.pallas_call(
            lambda *refs: first_kernel(*refs, far=is_far),
            out_shape=(shape((2, GROUP * tok, HD), F32), shape((GROUP * tok, HD), F32)),
            in_specs=[SMEM] * 2 + [VMEM] * 7,
            out_specs=(VMEM, VMEM),
            compiler_params=params(),
            cost_estimate=cost(4),
        )(span_count, prompt_len, queries, p0, p1, p2, p3, a, b)

    def last(queries, is_far, dtype, state):
        return call(
            lambda *refs: last_kernel(*refs, far=is_far),
            shape((tok, wide), dtype),
            [SMEM] + [VMEM] * 5,
            4,
            span_count,
            queries,
            c,
            d,
            *state,
        )

    far_state, near_state = first(bundle, 1), first(prompt_q, 0)
    c, far_state, near_state = lax.optimization_barrier((c, far_state, near_state))
    d = lax.ppermute(c, "c", SWAP)

    lanes = a.shape[0]
    last_units = pl.BlockSpec((lanes, 2, UNIT, HD), lambda i: (0, slots // 4, 0, 0))
    terms = pl.pallas_call(
        project_kernel,
        out_shape=shape((4, prompts * steps // 4, w_out.shape[1]), F32),
        grid=(1,),
        in_specs=[last_units] * 2 + [whole(w_out)],
        out_specs=pl.BlockSpec((4, prompts * steps // 4, w_out.shape[1]), lambda i: (0, 0, 0)),
        scratch_shapes=[pltpu.VMEM((prompts * steps, w_out.shape[1]), F32)],
        compiler_params=params(),
        cost_estimate=cost(1),
    )(a, c, w_out)
    given = lax.ppermute(jnp.stack([terms[1], terms[2]]), "x", [(i, i ^ 1) for i in range(4)])
    far_out = last(bundle, 1, BF16, far_state)
    prompt_q, far_out, terms, given = lax.optimization_barrier((prompt_q, far_out, terms, given))
    far_out = lax.ppermute(far_out, "hi", SWAP)
    near_out = last(prompt_q, 0, F32, near_state)
    near_out, summed = lax.optimization_barrier((near_out, terms[3] + given[1]))
    rest = lax.ppermute(summed, "x", [(i, i ^ 3) for i in range(4)])
    far_out = far_out.astype(F32)
    low = hi == 0
    prefill_out = jnp.concatenate(
        [jnp.where(low, near_out, far_out), jnp.where(low, far_out, near_out)], axis=1
    )[None]
    prefill_out, rest = lax.optimization_barrier((prefill_out, rest))
    decode_out = (terms[0] + given[0] + rest).astype(BF16)
    return prefill_out, decode_out


def solution(mesh):
    fine = Mesh(mesh.devices.reshape(2, 2, 2, 4, 4, 2), ("hi", "lo", "c", "x", "y", "zh"))
    store = ("hi", "lo", "c")
    owners = store + DECODE
    placed = (
        P(DECODE, store, "x"),
        P(DECODE, store, "x"),
        P(DECODE, store, "x"),
        P(owners, None, "x"),
        P(owners, None, "x"),
        P(owners, "x"),
        P(owners, "x"),
        P(),
        P(),
        P(),
        P(),
        P(None, None, "x"),
        P(None, None, "x"),
        P(None, None, "x"),
        P("x", owners),
    )
    return jax.shard_map(
        on_device,
        mesh=fine,
        in_specs=placed,
        out_specs=(P(DECODE, store, "x"), P("x", owners)),
        check_vma=False,
    )
```

```python
import math

import jax
import jax.numpy as jnp
from jax import lax
from jax.experimental import pallas as pl
from jax.experimental.pallas import tpu as pltpu
from jax.sharding import Mesh, PartitionSpec as P

NEG = -1e30
HD = 128
GROUP = 8
UNIT = 16
VMEM = pl.BlockSpec(memory_space=pltpu.VMEM)
SMEM = pl.BlockSpec(memory_space=pltpu.SMEM)
RANKS = ("hi", "lo", "y", "zh")
DECODE = ("y", "zh")
SWAP = [(0, 1), (1, 0)]
COEF = math.log2(math.e) / math.sqrt(HD)
BF16 = jnp.bfloat16
F32 = jnp.float32


def params(limit=40):
    return pltpu.CompilerParams(vmem_limit_bytes=limit << 20)


def cost(us):
    return pl.CostEstimate(flops=int(us * 1.1e9), bytes_accessed=1 << 16, transcendentals=0)


def call(kernel, out_shape, in_specs, us, *args):
    return pl.pallas_call(
        kernel,
        out_shape=out_shape,
        in_specs=in_specs,
        out_specs=VMEM,
        compiler_params=params(),
        cost_estimate=cost(us),
    )(*args)


def whole(x):
    return pl.BlockSpec(x.shape, lambda i: (0,) * len(x.shape))


def single(kernel, out, scalars, us, args, scratch=(), limit=40):
    return pl.pallas_call(
        kernel,
        grid=(1,),
        out_shape=out,
        in_specs=[SMEM] * scalars + [whole(x) for x in args[scalars:]],
        out_specs=whole(out),
        scratch_shapes=list(scratch),
        compiler_params=params(limit),
        cost_estimate=cost(us),
    )(*args)


def lane_of_decode():
    return lax.axis_index("y") * 2 + lax.axis_index("zh")


def scores_of(queries, keys):
    return lax.dot_general(queries, keys, (((1,), (1,)), ((), ())), preferred_element_type=F32)


def iota(shape, dim):
    return lax.broadcasted_iota(jnp.int32, shape, dim)


def pack_kernel(q, out):
    wide = GROUP * HD
    out[...] = q[0, :, pl.ds(pl.multiple_of((1 - lax.axis_index("hi")) * wide, wide), wide)]


def pack_keys_kernel(k, v, out):
    at = pl.ds(pl.multiple_of((1 - lax.axis_index("hi")) * HD, HD), HD)
    out[0] = k[0, :, at]
    out[1] = v[0, :, at]


def pair_kernel(k, v, bundle, out):
    at = pl.ds(pl.multiple_of(lax.axis_index("hi") * HD, HD), HD)
    out[0, 0] = k[0, :, at]
    out[1, 0] = v[0, :, at]
    out[0, 1] = bundle[0]
    out[1, 1] = bundle[1]


def spread_kernel(
    counts, lengths, k_scale, v_scale, span_k, span_v, prompt_k, prompt_v, span_list, span_slot, decode_q, new_k, new_v, out, fresh, dq
):
    tok = prompt_k.shape[1]
    prompts, steps = new_k.shape[:2]
    rows = prompts * steps
    lane = lane_of_decode()
    place = lax.axis_index("hi") * 4 + lax.axis_index("lo") * 2 + lax.axis_index("c")
    keys, values = [], []
    for kind, (codes, scale, full) in enumerate(((span_k, k_scale, keys), (span_v, v_scale, values))):
        factors = scale[...].astype(F32)
        for head in range(2):
            full.append([])
            for block in range(2):
                part = codes[block, :, head * HD : (head + 1) * HD].astype(F32)
                part = (part * factors[block : block + 1, head : head + 1]).astype(BF16)
                full[head].append(part)
                units = part.reshape(2, 4, UNIT, HD)
                for half in range(2):
                    for y in range(4):
                        out[head, half, 2 * y + kind, block] = units[half, y]
    for p in range(prompts):
        dq[p * steps : (p + 1) * steps] = decode_q[p].astype(F32)
    fresh[...] = jnp.zeros_like(fresh)
    fresh[0, 0:steps] = new_k[lane].astype(F32)
    fresh[1, 0:steps] = new_v[lane].astype(F32)
    width = 4 * HD
    row = iota((rows, 1), 0)
    prompt = row // steps
    step = row % steps
    listed = jnp.zeros((rows, span_list.shape[1]), jnp.int32)
    used = jnp.zeros((rows, 1), jnp.int32)
    for p in range(prompts):
        listed = jnp.where(prompt == p, span_list[p : p + 1, :], listed)
        used = jnp.where(prompt == p, counts[p], used)
    live = iota(listed.shape, 1) < used
    col = iota((rows, width), 1)
    slot = span_slot[...]
    first = (place * prompts + lane) * 2
    keep = jnp.zeros((rows, width), jnp.int32)
    for block in range(2):
        name = jnp.sum(jnp.where(slot == first + block, iota(slot.shape, 1), 0), axis=1, keepdims=True)
        has = jnp.max(jnp.where(live & (listed == name), 1, 0), axis=1, keepdims=True)
        keep = jnp.where((col >> 7) == block, has, keep)
    mine = jnp.where(prompt == lane, 1, 0)
    at = col - 2 * HD
    old = jnp.where((at >= 0) & (at < tok) & (place * tok + at < lengths[lane]), 1, 0)
    new = jnp.where((at >= HD) & (at - HD <= step) & (place == 0), 1, 0)
    keep = jnp.where(at >= 0, (old | new) * mine, keep)
    keep = (keep > 0)[None]
    for head in range(2):
        lanes = slice(head * HD, (head + 1) * HD)
        gap = jnp.zeros((HD - tok, HD), BF16)
        k_all = jnp.concatenate(keys[head] + [prompt_k[0, :, lanes], gap, fresh[0, :, lanes].astype(BF16)], axis=0)
        v_all = jnp.concatenate(values[head] + [prompt_v[0, :, lanes], gap, fresh[1, :, lanes].astype(BF16)], axis=0)
        base = head * GROUP
        queries = jnp.concatenate([dq[:, (base + g) * HD : (base + g + 1) * HD] for g in range(GROUP)], axis=0).astype(BF16)
        scores = scores_of(queries, k_all).reshape(GROUP, rows, width)
        scores = jnp.where(keep, scores, NEG) * COEF
        peak = jnp.max(scores, axis=2, keepdims=True)
        peak_hi = peak.astype(BF16).astype(F32)
        peak_lo = (peak - peak_hi).astype(BF16).astype(F32)
        weights = jnp.where(keep, jnp.exp2(scores - (peak_hi + peak_lo)), 0.0)
        total = jnp.sum(weights, axis=2, keepdims=True)
        total_hi = total.astype(BF16).astype(F32)
        total_lo = total - total_hi
        accum = jnp.dot(weights.reshape(GROUP * rows, width).astype(BF16), v_all, preferred_element_type=F32)
        accum = accum.astype(BF16).reshape(GROUP, 2, UNIT, HD)
        at = iota((GROUP, rows, HD), 2)
        stats = jnp.where(at == 0, peak_hi, jnp.where(at == 1, peak_lo, jnp.where(at == 2, total_hi, total_lo)))
        stats = jnp.where(at < 4, stats, 0.0).astype(BF16).reshape(GROUP, 2, UNIT, HD)
        for half in range(2):
            out[head, half, :, 2] = accum[:, half]
            out[head, half, :, 3] = stats[:, half]


def combine_kernel(mine, other, out):
    count = mine.shape[0]
    stats = jnp.concatenate([x[:, 3].reshape(count * UNIT, HD) for x in (mine, other)], axis=0)
    row, col = iota((HD, 2 * HD), 0), iota((HD, 2 * HD), 1)
    spread = jnp.where((row < 4) & ((row >> 1) == (col >> 7)), 1.0, 0.0).astype(BF16)
    stats = jnp.dot(stats, spread, preferred_element_type=F32)
    peaks = stats[:, :HD].reshape(2, count, UNIT, HD)
    totals = stats[:, HD:].reshape(2, count, UNIT, HD)
    share = jnp.exp2(peaks - jnp.max(peaks, axis=(0, 1), keepdims=True))
    total = jnp.sum(totals * share, axis=(0, 1))
    accum = jnp.sum(mine[:, 2].astype(F32) * share[0], axis=0) + jnp.sum(other[:, 2].astype(F32) * share[1], axis=0)
    out[...] = (accum / total).astype(BF16)


def choose_kernel(span_list, span_slot, mine, other, near, far, out, held):
    core, hi = lax.axis_index("c"), lax.axis_index("hi")
    slots = out.shape[1] - 2
    held[0] = mine[:, 0:2]
    held[1] = other[:, 0:2]
    for p in range(out.shape[0]):
        for t in range(slots):
            block = span_slot[span_list[p, 2 * t + core]]
            source = ((block >> 5) << 3) | ((block >> 1) & 7)
            out[p, t] = held[((block >> 4) & 1) ^ core, source, block & 1]
        out[p, slots + hi] = near[...]
        out[p, slots + 1 - hi] = far[...]


def begin(scores, values):
    peak = jnp.max(scores, axis=1, keepdims=True)
    weights = jnp.exp2(scores * COEF - peak * COEF)
    total = jnp.sum(weights, axis=1, keepdims=True)
    accum = jnp.dot(weights.astype(BF16), values, preferred_element_type=F32)
    return peak, total, accum


def extend(state, scores, values):
    high, total, accum = state
    peak = jnp.maximum(high, jnp.max(scores, axis=1, keepdims=True))
    shrink = jnp.exp2((high - peak) * COEF)
    weights = jnp.exp2(scores * COEF - peak * COEF)
    total = total * shrink + jnp.sum(weights, axis=1, keepdims=True)
    accum = accum * shrink + jnp.dot(weights.astype(BF16), values, preferred_element_type=F32)
    return peak, total, accum


PART = 4


def doc_rows(ref, kind, first):
    parts = [ref[2 * y + kind, pl.ds(first, PART)].reshape(PART * UNIT, HD) for y in range(4)]
    return jnp.concatenate(parts, axis=0)


def over_documents(queries, state, count, own, other):
    core = lax.axis_index("c")
    slots = own.shape[1] - 2
    col = iota((1, 8 * PART * UNIT), 1)
    parity = core ^ (col // (4 * PART * UNIT))
    turn = (col // UNIT) & (PART - 1)

    def one(i, state):
        first = jnp.minimum(PART * i, slots - PART)
        keys = jnp.concatenate([doc_rows(own, 0, first), doc_rows(other, 0, first)], axis=0)
        values = jnp.concatenate([doc_rows(own, 1, first), doc_rows(other, 1, first)], axis=0)
        at = first + turn
        bias = jnp.where((at >= PART * i) & (2 * at + parity < count), 0.0, NEG)
        return extend(state, scores_of(queries, keys) + bias, values)

    return lax.fori_loop(0, (count + 2 * PART - 1) // (2 * PART), one, state)


def queries_of(q, far):
    wide = GROUP * HD
    if far:
        heads = [q[:, g * HD : (g + 1) * HD] for g in range(GROUP)]
    else:
        base = lax.axis_index("hi") * wide
        heads = [q[0, :, pl.ds(pl.multiple_of(base + g * HD, HD), HD)] for g in range(GROUP)]
    return jnp.concatenate(heads, axis=0)


def first_kernel(counts, lengths, q, p0, p1, p2, p3, a, b, stats, sums, *, far):
    hi, lo, core = lax.axis_index("hi"), lax.axis_index("lo"), lax.axis_index("c")
    lane = lane_of_decode()
    count, length = counts[lane], lengths[lane]
    rows = sums.shape[0]
    tok = rows // GROUP
    col = iota((1, 8 * tok), 1)
    kpos = ((core ^ (col >> 8)) << 6) | ((lo ^ ((col >> 7) & 1)) << 7) | ((hi ^ ((col >> 6) & 1)) << 8) | (col & 63)
    row = iota((rows, 1), 0)
    pkeys = jnp.concatenate([x[0].reshape(2 * tok, HD) for x in (p0, p1, p2, p3)], axis=0)
    pvalues = jnp.concatenate([x[1].reshape(2 * tok, HD) for x in (p0, p1, p2, p3)], axis=0)
    queries = queries_of(q, far)
    qpos = (((hi ^ far) << 2) | (lo << 1) | core) * tok + (row & (tok - 1))
    keep = (kpos <= qpos) & (kpos < length)
    state = begin(jnp.where(keep, scores_of(queries, pkeys), NEG), pvalues)
    peak, total, accum = over_documents(queries, state, count, a, b)
    sums[...] = accum
    stats[0] = jnp.broadcast_to(peak, sums.shape)
    stats[1] = jnp.broadcast_to(total, sums.shape)


def last_kernel(counts, q, c, d, stats, sums, out, *, far):
    count = counts[lane_of_decode()]
    tok = out.shape[0]
    queries = queries_of(q, far)
    peak = jnp.max(stats[0], axis=1, keepdims=True)
    total = jnp.max(stats[1], axis=1, keepdims=True)
    state = (peak, total, sums[...])
    _, total, accum = over_documents(queries, state, count, c, d)
    result = (accum / total).astype(out.dtype)
    for g in range(GROUP):
        out[:, g * HD : (g + 1) * HD] = result[g * tok : (g + 1) * tok]


def project_kernel(own, swapped, w, out, held):
    lo, mine = lax.axis_index("lo"), lax.axis_index("x")

    def rows(x):
        return jnp.concatenate([x[g, head] for head in range(2) for g in range(GROUP)], axis=1)

    terms = jnp.dot(jnp.concatenate([rows(own), rows(swapped)], axis=0), w[...], preferred_element_type=F32)
    held[pl.ds(pl.multiple_of(lo * UNIT, UNIT), UNIT)] = terms[:UNIT]
    held[pl.ds(pl.multiple_of((1 - lo) * UNIT, UNIT), UNIT)] = terms[UNIT:]
    piece = out.shape[1]
    for k in range(4):
        out[k] = held[pl.ds(pl.multiple_of((mine ^ k) * piece, piece), piece)]


def on_device(
    prompt_q,
    prompt_k,
    prompt_v,
    span_k,
    span_v,
    k_scale,
    v_scale,
    span_list,
    span_slot,
    span_count,
    prompt_len,
    decode_q,
    new_k,
    new_v,
    w_out,
):
    hi = lax.axis_index("hi")
    tok = prompt_q.shape[1]
    prompts, steps = decode_q.shape[:2]
    slots = span_list.shape[1]
    wide = GROUP * HD
    shape = jax.ShapeDtypeStruct

    payload = single(
        spread_kernel,
        shape((2, 2, 8, 4, UNIT, HD), BF16),
        2,
        5,
        (
            span_count,
            prompt_len,
            k_scale,
            v_scale,
            span_k,
            span_v,
            prompt_k,
            prompt_v,
            span_list,
            span_slot.reshape(1, -1),
            decode_q,
            new_k,
            new_v,
        ),
        [pltpu.VMEM((2, HD, 2 * HD), F32), pltpu.VMEM((prompts * steps, decode_q.shape[2]), F32)],
        limit=60,
    )
    mine = lax.all_to_all(payload.reshape(32, 4, UNIT, HD), RANKS, 0, 0, tiled=True)
    bundle = single(pack_kernel, shape((tok, wide), BF16), 0, 1.5, (prompt_q,), limit=60)
    pairs = single(pack_keys_kernel, shape((2, tok, HD), BF16), 0, 1, (prompt_k, prompt_v), limit=60)
    pairs = lax.ppermute(pairs, "hi", SWAP)
    mine, bundle, pairs = lax.optimization_barrier((mine, bundle, pairs))
    bundle = lax.ppermute(bundle, "hi", SWAP)
    other = lax.ppermute(mine, "c", SWAP)

    done = call(combine_kernel, shape((UNIT, HD), BF16), [VMEM] * 2, 1, mine, other)
    chosen = pl.pallas_call(
        choose_kernel,
        out_shape=shape((prompts, slots // 2 + 2, UNIT, HD), BF16),
        in_specs=[SMEM] * 2 + [VMEM] * 4,
        out_specs=VMEM,
        scratch_shapes=[pltpu.VMEM((2, 32, 2, UNIT, HD), BF16)],
        compiler_params=params(),
        cost_estimate=cost(1),
    )(span_list, span_slot, mine, other, done, lax.ppermute(done, "hi", SWAP))
    p0 = single(pair_kernel, shape((2, 2, tok, HD), BF16), 0, 1.5, (prompt_k, prompt_v, pairs))
    p1 = lax.ppermute(p0, "lo", SWAP)
    p2 = lax.ppermute(p0, "c", SWAP)
    p3 = lax.ppermute(p1, "c", SWAP)
    a = lax.all_to_all(chosen, DECODE, 0, 0, tiled=True)
    a, p1, p2, p3, bundle = lax.optimization_barrier((a, p1, p2, p3, bundle))
    c = lax.ppermute(a, "lo", SWAP)
    b = lax.ppermute(a, "c", SWAP)

    def first(queries, is_far):
        return pl.pallas_call(
            lambda *refs: first_kernel(*refs, far=is_far),
            out_shape=(shape((2, GROUP * tok, HD), F32), shape((GROUP * tok, HD), F32)),
            in_specs=[SMEM] * 2 + [VMEM] * 7,
            out_specs=(VMEM, VMEM),
            compiler_params=params(),
            cost_estimate=cost(4),
        )(span_count, prompt_len, queries, p0, p1, p2, p3, a, b)

    def last(queries, is_far, dtype, state):
        return call(
            lambda *refs: last_kernel(*refs, far=is_far),
            shape((tok, wide), dtype),
            [SMEM] + [VMEM] * 5,
            4,
            span_count,
            queries,
            c,
            d,
            *state,
        )

    far_state, near_state = first(bundle, 1), first(prompt_q, 0)
    c, far_state, near_state = lax.optimization_barrier((c, far_state, near_state))
    d = lax.ppermute(c, "c", SWAP)

    lanes = a.shape[0]
    last_units = pl.BlockSpec((lanes, 2, UNIT, HD), lambda i: (0, slots // 4, 0, 0))
    terms = pl.pallas_call(
        project_kernel,
        out_shape=shape((4, prompts * steps // 4, w_out.shape[1]), F32),
        grid=(1,),
        in_specs=[last_units] * 2 + [whole(w_out)],
        out_specs=pl.BlockSpec((4, prompts * steps // 4, w_out.shape[1]), lambda i: (0, 0, 0)),
        scratch_shapes=[pltpu.VMEM((prompts * steps, w_out.shape[1]), F32)],
        compiler_params=params(),
        cost_estimate=cost(1),
    )(a, c, w_out)
    given = lax.ppermute(jnp.stack([terms[1], terms[3]]), "x", [(i, i ^ 1) for i in range(4)])
    far_out = last(bundle, 1, BF16, far_state)
    prompt_q, far_out, terms, given = lax.optimization_barrier((prompt_q, far_out, terms, given))
    far_out = lax.ppermute(far_out, "hi", SWAP)
    near_out = last(prompt_q, 0, F32, near_state)
    near_out, summed = lax.optimization_barrier((near_out, terms[2] + given[1]))
    rest = lax.ppermute(summed, "x", [(i, i ^ 2) for i in range(4)])
    far_out = far_out.astype(F32)
    low = hi == 0
    prefill_out = jnp.concatenate(
        [jnp.where(low, near_out, far_out), jnp.where(low, far_out, near_out)], axis=1
    )[None]
    prefill_out, rest = lax.optimization_barrier((prefill_out, rest))
    decode_out = (terms[0] + given[0] + rest).astype(BF16)
    return prefill_out, decode_out


def solution(mesh):
    fine = Mesh(mesh.devices.reshape(2, 2, 2, 4, 4, 2), ("hi", "lo", "c", "x", "y", "zh"))
    store = ("hi", "lo", "c")
    owners = store + DECODE
    placed = (
        P(DECODE, store, "x"),
        P(DECODE, store, "x"),
        P(DECODE, store, "x"),
        P(owners, None, "x"),
        P(owners, None, "x"),
        P(owners, "x"),
        P(owners, "x"),
        P(),
        P(),
        P(),
        P(),
        P(None, None, "x"),
        P(None, None, "x"),
        P(None, None, "x"),
        P("x", owners),
    )
    return jax.shard_map(
        on_device,
        mesh=fine,
        in_specs=placed,
        out_specs=(P(DECODE, store, "x"), P("x", owners)),
        check_vma=False,
    )
```
